32 devices in a mesh: wide: 4 (over z), mid: 4 (over y, core), low: 2 (over x).
Axes of the slice: x: 2, y: 2, z: 4, core: 2. Of those that a mesh axis runs over, the one named last changes fastest.
Arguments:
- state: float32 [2, 4, 4, 2, 16384], P(None, 'wide', 'mid', 'low'), may hold values from -6 to 6
- gates: float32 [10, 2, 128, 128], replicated, may hold values from -0.375 to 0.375
- phase_low: float32 [128], replicated, may hold values from -3.140625 to 3.140625
- phase_mid: float32 [128], replicated, may hold values from -3.140625 to 3.140625
- phase_top: float32 [4, 4, 2, 1], P('wide', 'mid', 'low'), may hold values from -3.140625 to 3.140625
- swap_qubits: int32 [2], replicated, may hold values from 0 to 2, as said below
- regroup_order: int32 [4], replicated, may hold values from 0 to 3, each once
Outputs:
- final_state: float32 [2, 4, 4, 2, 16384], P(None, 'wide', 'mid', 'low')
The draws below stay inside these ranges and needn't reach their ends.
Inputs may be any that keep to these rules, and one draw needn't show every extreme that they name: `swap_qubits`: the two entries differ, and one of them is 2. `regroup_order`: each of 0 to 3 once.
All inputs are finite; a program needn't handle non-finite values.
Results may differ from the reference program's by a relative error of at most 0.0003.
Values sent between devices are 32-bit elements; how exact they have to be, the bound alone decides.
No kernel may reach another device: no remote copies, remote signals or barrier semaphores. Data moves between devices by JAX's collectives and lax.ppermute only.
A program may use at most 64 MiB of HBM per device.

```python
from functools import partial
import jax
import jax.numpy as jnp
from jax import lax

NG = 10
LQ = 14
WQ = 2
GATE = 128
UPPER = 1
LOCAL = 16384
N_WIDE = 4
N_MID = 4
N_LOW = 2


def draw_swap_qubits(key, part):
    folded = jax.random.fold_in(key, 11)
    first_key, second_key = jax.random.split(folded)
    where_two = jax.random.randint(first_key, (), 0, 2, dtype=jnp.int32)
    other_value = jax.random.randint(second_key, (), 0, 2, dtype=jnp.int32)
    places = jnp.arange(2, dtype=jnp.int32)
    return jnp.where(places == where_two, jnp.int32(2), other_value).astype(jnp.int32)


def block_levels(stream_key, dims, cuts, smallest, top_value):
    def one(position, blocks):
        steps = jax.random.uniform(jax.random.fold_in(jax.random.fold_in(stream_key, 6), position), (blocks,), jnp.float32, smallest / len(cuts), top_value / len(cuts))
        return jnp.repeat(jnp.exp(steps), dims[position] // blocks).reshape((-1,) + (1,) * (len(dims) - position - 1))

    level = one(*cuts[0])
    for cut in cuts[1:]:
        level = level * one(*cut)
    return level


def gaussian(key, extent, width, bound, cuts=(), kind=jnp.bfloat16):
    values = width * jax.random.normal(key, extent, jnp.float32)
    if cuts:
        values = values * block_levels(key, extent, cuts, -0.22, 0.18)
    return jnp.clip(values, -bound, bound).astype(kind)


def setup_inputs(seed: int = 0) -> dict:
    streams_of = jax.random.split(jax.random.key(seed), 8)
    state = gaussian(streams_of[0], (2, N_WIDE, N_MID, N_LOW, LOCAL), 1.0, 6.0, ((1, 4), (2, 4), (3, 2)), jnp.float32)
    gates = gaussian(streams_of[1], (NG, 2, GATE, GATE), (2 * GATE) ** -0.5, 0.375, (), jnp.float32)
    phase_low = jnp.clip(jax.random.uniform(streams_of[2], (GATE,), jnp.float32, -3.140625, 3.140625), -3.140625, 3.140625)
    phase_mid = jnp.clip(jax.random.uniform(streams_of[3], (GATE,), jnp.float32, -3.140625, 3.140625), -3.140625, 3.140625)
    phase_top = jnp.clip(jax.random.uniform(streams_of[4], (N_WIDE, N_MID, N_LOW, UPPER), jnp.float32, -3.140625, 3.140625), -3.140625, 3.140625)
    swap_qubits = draw_swap_qubits(jax.random.fold_in(streams_of[7], 71), 0)
    regroup_order = jax.random.permutation(streams_of[6], 4).astype(jnp.int32)
    return dict(state=state, gates=gates, phase_low=phase_low, phase_mid=phase_mid, phase_top=phase_top, swap_qubits=swap_qubits, regroup_order=regroup_order)


HIGH = lax.Precision.HIGHEST


def gate_inner(vector, real_gate, imag_gate):
    def product(values, matrix):
        return jnp.einsum('...b,ab->...a', values, matrix, precision=HIGH)
    real_part, imag_part = vector[0], vector[1]
    return jnp.stack([product(real_part, real_gate) - product(imag_part, imag_gate),
                      product(real_part, imag_gate) + product(imag_part, real_gate)])


def gate_outer(vector, real_gate, imag_gate):
    def product(values, matrix):
        return jnp.einsum('ab,rbc->rac', matrix, values, precision=HIGH)
    real_part, imag_part = vector[0], vector[1]
    return jnp.stack([product(real_part, real_gate) - product(imag_part, imag_gate),
                      product(real_part, imag_gate) + product(imag_part, real_gate)])


def apply_gate(vector, gates, number):
    if number % 2 == 0:
        result = gate_inner(vector.reshape(2, -1, GATE), gates[number, 0], gates[number, 1])
    else:
        result = gate_outer(vector.reshape(2, -1, GATE, GATE), gates[number, 0], gates[number, 1])
    return result.reshape(2, -1)


def pair_swap(vector, outer_count, inner_count, qubit):
    shaped = vector.reshape(2, outer_count, 2, inner_count, LOCAL >> (qubit + 1), 2, 2 ** qubit)
    shaped = jnp.swapaxes(shaped, 2, 5)
    return shaped.reshape(vector.shape)


def reference(state, gates, phase_low, phase_mid, phase_top, swap_qubits, regroup_order):
    device_count = N_WIDE * N_MID * N_LOW
    vector = apply_gate(state.reshape(2, -1), gates, 0)
    vector = vector.reshape(2, device_count, UPPER, GATE, GATE)
    angle = (phase_top.reshape(device_count, UPPER)[:, :, None, None]
             + phase_mid[None, None, :, None] + phase_low[None, None, None, :])
    cosine = jnp.cos(angle)
    sine_part = jnp.sin(angle)
    vector = jnp.stack([vector[0] * cosine - vector[1] * sine_part,
                        vector[0] * sine_part + vector[1] * cosine]).reshape(2, -1)
    for number in range(1, 4):
        vector = apply_gate(vector, gates, number)
    vector = vector.reshape(2, device_count, LOCAL)
    mid_branches = [partial(pair_swap, outer_count=N_WIDE * (N_MID // 2), inner_count=N_LOW, qubit=LQ - 3 + place) for place in range(3)]
    vector = lax.switch(swap_qubits[0], mid_branches, vector)
    row_ids = jnp.arange(16, dtype=jnp.int32)[:, None]
    row_bits = jnp.right_shift(row_ids, jnp.arange(4, dtype=jnp.int32)[None, :]) & 1
    row_index = jnp.sum(jnp.left_shift(row_bits, regroup_order[None, :]), axis=1).astype(jnp.int32)
    vector = jnp.take(vector.reshape(2, device_count, 16, LOCAL // 16), row_index, axis=2)
    vector = vector.reshape(2, device_count, LOCAL)
    low_branches = [partial(pair_swap, outer_count=N_WIDE * N_MID * (N_LOW // 2), inner_count=1, qubit=LQ - WQ - 3 + place) for place in range(3)]
    vector = lax.switch(swap_qubits[1], low_branches, vector)
    vector = vector.reshape(2, N_WIDE, N_MID * N_LOW, N_WIDE, LOCAL // N_WIDE)
    vector = jnp.swapaxes(vector, 1, 3).reshape(2, -1)
    for number in range(4, NG):
        vector = apply_gate(vector, gates, number)
    return vector.reshape(state.shape)
```

```python
from functools import partial

import jax
import jax.numpy as jnp
from jax import lax
from jax.experimental import pallas as pl
from jax.experimental.pallas import tpu as pltpu
from jax.sharding import PartitionSpec as P

HIGH = lax.Precision.HIGHEST
AXES = ("wide", "mid", "low")
VSPEC = pl.BlockSpec(memory_space=pltpu.VMEM)
SSPEC = pl.BlockSpec(memory_space=pltpu.SMEM)


def split(value):
    high = value.astype(jnp.bfloat16)
    return high, (value - high.astype(jnp.float32)).astype(jnp.bfloat16)


def embed(value):
    half = value.shape[1] // 2
    return jnp.concatenate([value, jnp.concatenate([-value[:, half:], value[:, :half]], 1)], 0)


def dot(left, right, transposed=False):
    dims = (((1,), (1 if transposed else 0,)), ((), ()))
    return lax.dot_general(left, right, dims, preferred_element_type=jnp.float32)


def product(left, right, transposed=False):
    rows = left[0].shape[0]
    both = dot(jnp.concatenate(left, 0), right[0], transposed)
    return both[:rows] + both[rows:] + dot(left[0], right[1], transposed)


def complex_product(left, right):
    return product(left, tuple(embed(part) for part in right))


def turn(value, angle):
    half = value.shape[1] // 2
    cosine, sine = jnp.cos(angle), jnp.sin(angle)
    real, imag = value[:, :half], value[:, half:]
    return jnp.concatenate([real * cosine - imag * sine, real * sine + imag * cosine], 1)


def side(ref):
    return jnp.concatenate([ref[0], ref[1]], 1)


class Plan:
    def __init__(self, rows, wide_count):
        self.rows = rows
        self.row_bits = rows.bit_length() - 1
        self.wide_bits = wide_count.bit_length() - 1
        self.low_base = self.row_bits - self.wide_bits - 3
        self.chunk = rows // (2 * wide_count)
        self.offsets = [wide_count - 1] + list(range(1, wide_count - 1))
        self.slots = len(self.offsets)

    def first(self, slot):
        return slot % 2


def pick(index, table):
    value = jnp.zeros_like(index)
    for place, entry in enumerate(table):
        value = jnp.where(index == place, entry, value)
    return value


def free_row(plan, inner, swap):
    base = plan.low_base
    lower = base + jnp.where(swap == 0, 1, 0)
    upper = base + jnp.where(swap == 2, 1, 2)
    return (
        (inner & ((1 << base) - 1))
        | jnp.left_shift(jnp.right_shift(inner, base) & 1, lower)
        | jnp.left_shift(jnp.right_shift(inner, base + 1) & 1, upper)
    )


def sent_rows(plan, index, swaps, order):
    wide, core, low = lax.axis_index("wide"), lax.axis_index("mid") & 1, lax.axis_index("low")
    block, inner = index // plan.chunk, index % plan.chunk
    wide_offsets, low_offsets, cores = [0], [0], [core]
    for slot, offset in enumerate(plan.offsets):
        wide_offsets += [offset, offset]
        low_offsets += [core ^ plan.first(slot)] * 2
        cores += [core, 1 - core]
    wide_offsets.append(0)
    low_offsets.append(1)
    cores.append(core)
    to_wide = wide ^ pick(block, wide_offsets)
    to_low = (low & 1) ^ pick(block, low_offsets)
    to_core = pick(block, cores)
    row = free_row(plan, inner, swaps[1])
    row |= jnp.left_shift(to_low, plan.low_base + swaps[1])
    row |= jnp.left_shift(to_wide, plan.row_bits - plan.wide_bits)
    base = plan.row_bits - 4
    old = row & ((1 << base) - 1)
    for place in range(4):
        old |= jnp.left_shift(jnp.right_shift(row, base + place) & 1, base + order[place])
    position = plan.row_bits - 3 + swaps[0]
    from_core = jnp.right_shift(old, position) & 1
    old = (old & ~jnp.left_shift(1, position)) | jnp.left_shift(to_core, position)
    return old, from_core


def received_rows(plan, index, swaps):
    wide, core, low = lax.axis_index("wide"), lax.axis_index("mid") & 1, lax.axis_index("low")
    block, inner = index // plan.chunk, index % plan.chunk
    wide_offsets = [0] + plan.offsets + [0] + plan.offsets
    low_offsets = [0] + [core ^ plan.first(slot) for slot in range(plan.slots)] + [1]
    low_offsets += [1 - (core ^ plan.first(slot)) for slot in range(plan.slots)]
    from_wide = wide ^ pick(block, wide_offsets)
    from_low = (low & 1) ^ pick(block, low_offsets)
    row = free_row(plan, inner, swaps[1])
    row |= jnp.left_shift(from_low, plan.low_base + swaps[1])
    return row | jnp.left_shift(from_wide, plan.row_bits - plan.wide_bits)


def fetch(pairs, sems):
    copies = [pltpu.make_async_copy(a, b, sems.at[place]) for place, (a, b) in enumerate(pairs)]
    for copy in copies:
        copy.start()
    return copies


def front_kernel(plan, gates, phase_mid, phase_top, state, swaps, order, own, high, low, *scratch):
    *buffers, sems = scratch
    sources = (swaps, order, gates.at[3], gates.at[1], phase_mid, state, phase_top)
    copies = fetch(list(zip(sources, buffers)), sems)
    swaps, order, gate_three, gate_one, phase_mid, state, phase_top = buffers
    copies[0].wait()
    copies[1].wait()
    rows = plan.rows
    index = lax.broadcasted_iota(jnp.int32, (rows, rows), 0)
    source, from_core = sent_rows(plan, index, swaps, order)
    chosen = (lax.broadcasted_iota(jnp.int32, (rows, rows), 1) == source).astype(jnp.bfloat16)
    copies[2].wait()
    outer = split(side(gate_three))
    outer = tuple(dot(chosen, part).astype(jnp.bfloat16) for part in outer)
    copies[3].wait()
    copies[4].wait()
    inner = turn(side(gate_one), phase_mid[...])
    merged = complex_product(outer, split(inner))
    mine = jnp.concatenate([from_core == (lax.axis_index("mid") & 1)] * 2, 1)
    zeros = jnp.zeros_like(merged)
    copies[5].wait()
    copies[6].wait()
    value = split(side(state))
    own[...] = turn(complex_product(split(jnp.where(mine, merged, zeros)), value), phase_top[...])
    high[...], low[...] = split(jnp.where(mine, zeros, merged))


def send_kernel(plan, own, high, low, state, phase_top, *sent):
    value = split(side(state))
    total = own[...] + turn(complex_product((high[...], low[...]), value), phase_top[...])
    start = 0
    for ref in sent:
        ref[...] = total[start : start + ref.shape[0]]
        start += ref.shape[0]


def back_kernel(plan, count, gates, phase_low, swaps, kept, right_high, right_low, left_high, left_low):
    del kept
    rows = plan.rows

    def gate(number):
        return split(side(gates.at[number]))

    def chain(numbers, value):
        for number in numbers:
            value = complex_product(gate(number), split(value))
        return value

    right = turn(side(gates.at[2]), phase_low[...])
    right = complex_product(split(right), gate(0))
    right = chain(range(4, count, 2), right)
    half = rows
    real, imag = right[:, :half], right[:, half:]
    right = jnp.concatenate(
        [jnp.concatenate([real, -imag], 1), jnp.concatenate([imag, real], 1)], 0
    )
    right_high[...], right_low[...] = split(right)
    index = lax.broadcasted_iota(jnp.int32, (rows, rows), 1)
    target = received_rows(plan, index, swaps)
    placed = (lax.broadcasted_iota(jnp.int32, (rows, rows), 0) == target).astype(jnp.bfloat16)
    first = tuple(
        jnp.concatenate([dot(part[:, :half], placed), dot(part[:, half:], placed)], 1)
        for part in gate(5)
    )
    left = complex_product(gate(7), tuple(part.astype(jnp.bfloat16) for part in first))
    left = chain(range(9, count, 2), left)
    left_high[...], left_low[...] = split(left)


def sort_kernel(plan, *refs):
    chunk = plan.chunk
    received, give = refs[: plan.slots], refs[-1]
    for slot, ref in enumerate(received):
        give[slot * chunk : (slot + 1) * chunk] = ref[chunk:]


def kept_kernel(plan, *refs):
    *parts, right_high, right_low, high, low = refs
    value = jnp.concatenate([ref[: plan.chunk] for ref in parts], 0)
    value = product(split(value), (right_high[...], right_low[...]), True)
    high[...], low[...] = split(value)


def last_kernel(plan, high, low, given, right_high, right_low, left_high, left_low, out):
    value = split(product(split(given[...]), (right_high[...], right_low[...]), True))
    value = tuple(jnp.concatenate([a[...], b], 0) for a, b in zip((high, low), value))
    result = complex_product((left_high[...], left_low[...]), value)
    half = plan.rows
    out[0] = result[:, :half]
    out[1] = result[:, half:]


def call(kernel, shapes, args, specs, flops=0, scratch=()):
    args = [
        pltpu.with_memory_space_constraint(arg, pltpu.VMEM) if spec is VSPEC else arg
        for arg, spec in zip(args, specs)
    ]
    return pl.pallas_call(
        kernel,
        out_shape=[pltpu.VMEM(shape, dtype) for shape, dtype in shapes],
        in_specs=[pl.BlockSpec() if spec is None else spec for spec in specs],
        out_specs=[VSPEC] * len(shapes),
        scratch_shapes=scratch,
        cost_estimate=pl.CostEstimate(flops=flops, bytes_accessed=1 << 17, transcendentals=0),
    )(*args)


def exchange(value, offset, cores=(0, 0), flip=0):
    wides, mids, lows = (lax.axis_size(axis) for axis in AXES)
    pairs = []
    for wide in range(wides):
        for mid in range(mids):
            for low in range(lows):
                source = (wide * mids + mid) * lows + low
                to = ((wide ^ offset) * mids + (mid ^ flip)) * lows + (low ^ cores[mid & 1])
                pairs.append((source, to))
    return lax.ppermute(value, AXES, pairs)


def merged_device(state, gates, phase_low, phase_mid, phase_top, swap_qubits, regroup_order):
    rows = gates.shape[-1]
    plan = Plan(rows, lax.axis_size("wide"))
    chunk = plan.chunk
    f32, bf16 = jnp.float32, jnp.bfloat16
    square = state.reshape(2, rows, rows)
    top = phase_top.reshape(1, 1)
    other = exchange(square, 0, flip=1)
    other_top = exchange(top, 0, flip=1)

    pair = pltpu.VMEM((2, rows, rows), f32)
    sources = (gates, phase_mid.reshape(1, rows), top, square, swap_qubits, regroup_order)
    buffers = [pltpu.SMEM(arg.shape, arg.dtype) for arg in sources[4:]]
    buffers += [pair, pair, pltpu.VMEM((1, rows), f32), pair, pltpu.VMEM((1, 1), f32)]
    own, high, low = call(
        partial(front_kernel, plan),
        [((rows, 2 * rows), f32), ((rows, 2 * rows), bf16), ((rows, 2 * rows), bf16)],
        sources,
        (pl.BlockSpec(memory_space=pl.ANY),) * len(sources),
        scratch=buffers + [pltpu.SemaphoreType.DMA((len(buffers),))],
    )
    shapes = [(chunk, 2 * rows)] + [(2 * chunk, 2 * rows)] * plan.slots + [(chunk, 2 * rows)]
    local, *sent = call(
        partial(send_kernel, plan),
        [(shape, f32) for shape in shapes],
        (own, high, low, other, other_top),
        (VSPEC,) * 5,
    )
    received = [
        exchange(value, offset, (plan.first(slot), 1 - plan.first(slot)))
        for slot, (value, offset) in enumerate(zip(sent, plan.offsets))
    ]
    received.append(exchange(sent[-1], 0, (1, 1)))
    wide_square = ((2 * rows, 2 * rows), bf16)
    tall = ((rows, 2 * rows), bf16)
    right_high, right_low, left_high, left_low = call(
        partial(back_kernel, plan, gates.shape[0]),
        [wide_square, wide_square, tall, tall],
        (gates, phase_low.reshape(1, rows), swap_qubits, local),
        (None, None, SSPEC, VSPEC),
        flops=6 * 24 * rows**3,
    )
    (give,) = call(
        partial(sort_kernel, plan),
        [((plan.slots * chunk, 2 * rows), f32)],
        received[:-1],
        (VSPEC,) * plan.slots,
    )
    given = exchange(give, 0, flip=1)
    kept_rows = (plan.slots + 2) * chunk
    high, low = call(
        partial(kept_kernel, plan),
        [((kept_rows, 2 * rows), bf16)] * 2,
        (local, *received, right_high, right_low),
        (VSPEC,) * (plan.slots + 4),
    )
    args = (high, low, given, right_high, right_low, left_high, left_low)
    out = pl.pallas_call(
        partial(last_kernel, plan),
        out_shape=jax.ShapeDtypeStruct((2, rows, rows), f32),
        in_specs=[VSPEC] * len(args),
    )(*[pltpu.with_memory_space_constraint(arg, pltpu.VMEM) for arg in args])
    return out.reshape(state.shape)


def partner(value, axis, stride):
    mask = 2**stride
    pairs = [(source, source ^ mask) for source in range(lax.axis_size(axis))]
    return lax.ppermute(value, axis, pairs)


def gate_inner(vector, real_gate, imag_gate):

    def product(values, matrix):
        return jnp.einsum("...b,ab->...a", values, matrix, precision=HIGH)

    real_part, imag_part = (vector[0], vector[1])
    return jnp.stack(
        [
            product(real_part, real_gate) - product(imag_part, imag_gate),
            product(real_part, imag_gate) + product(imag_part, real_gate),
        ]
    )


def gate_outer(vector, real_gate, imag_gate):

    def product(values, matrix):
        return jnp.einsum("ab,rbc->rac", matrix, values, precision=HIGH)

    real_part, imag_part = (vector[0], vector[1])
    return jnp.stack(
        [
            product(real_part, real_gate) - product(imag_part, imag_gate),
            product(real_part, imag_gate) + product(imag_part, real_gate),
        ]
    )


def apply_gate(vector, gates, number, gate_len):
    if number % 2 == 0:
        result = gate_inner(vector.reshape(2, -1, gate_len), gates[number, 0], gates[number, 1])
    else:
        result = gate_outer(
            vector.reshape(2, -1, gate_len, gate_len), gates[number, 0], gates[number, 1]
        )
    return result.reshape(2, -1)


def half_rows(vector, offset, base, own_bit, local_len):
    counter = jnp.arange(4, dtype=jnp.int32)
    lower = counter & jnp.left_shift(1, offset) - 1
    higher = jnp.right_shift(counter, offset)
    row_index = jnp.left_shift(higher, offset + 1) | jnp.left_shift(1 - own_bit, offset) | lower
    blocks = vector.reshape(2, local_len >> base + 3, 8, 1 << base)
    return (blocks, row_index, jnp.take(blocks, row_index, axis=2))


def move_bits(vector, lower, upper, local_len):
    if lower == upper:
        return vector
    shaped = vector.reshape(2, local_len >> upper + 1, 2, 1 << upper - lower - 1, 2, 1 << lower)
    return jnp.swapaxes(shaped, 2, 4).reshape(2, local_len)


def general_device(state, gates, phase_low, phase_mid, phase_top, swap_qubits, regroup_order):
    local_len = state.shape[-1]
    gate_len = gates.shape[-1]
    gate_count = gates.shape[0]
    local_bits = local_len.bit_length() - 1
    upper_len = local_len // (gate_len * gate_len)
    wide_count = lax.axis_size("wide")
    wide_bits = wide_count.bit_length() - 1
    vector = apply_gate(state.reshape(2, -1), gates, 0, gate_len)
    vector = vector.reshape(2, upper_len, gate_len, gate_len)
    angle = (
        phase_top.reshape(upper_len)[:, None, None]
        + phase_mid[None, :, None]
        + phase_low[None, None, :]
    )
    cosine = jnp.cos(angle)
    sine_part = jnp.sin(angle)
    vector = jnp.stack(
        [vector[0] * cosine - vector[1] * sine_part, vector[0] * sine_part + vector[1] * cosine]
    ).reshape(2, -1)
    for number in range(1, 4):
        vector = apply_gate(vector, gates, number, gate_len)
    mid_bit = lax.axis_index("mid") & 1
    blocks, row_index, sent_half = half_rows(
        vector, swap_qubits[0], local_bits - 3, mid_bit, local_len
    )
    received = partner(sent_half, "mid", 0)
    vector = blocks.at[:, :, row_index].set(received).reshape(2, local_len)
    row_ids = jnp.arange(16, dtype=jnp.int32)[:, None]
    row_bits = jnp.right_shift(row_ids, jnp.arange(4, dtype=jnp.int32)[None, :]) & 1
    order_index = jnp.sum(jnp.left_shift(row_bits, regroup_order[None, :]), axis=1)
    vector = jnp.take(vector.reshape(2, 16, local_len // 16), order_index, axis=1).reshape(
        2, local_len
    )
    low_base = local_bits - wide_bits - 3
    target = low_base + 2
    branches = [
        partial(move_bits, lower=low_base + place, upper=target, local_len=local_len)
        for place in range(3)
    ]
    vector = lax.switch(swap_qubits[1], branches, vector)
    shaped = vector.reshape(2, wide_count, 2, local_len // (2 * wide_count))
    moved = lax.all_to_all(
        lax.all_to_all(shaped, "wide", split_axis=1, concat_axis=1, tiled=True),
        "low",
        split_axis=2,
        concat_axis=2,
        tiled=True,
    )
    vector = lax.switch(swap_qubits[1], branches, moved.reshape(2, local_len))
    for number in range(4, gate_count):
        vector = apply_gate(vector, gates, number, gate_len)
    return vector.reshape(state.shape)


def on_device(state, gates, *rest):
    rows = gates.shape[-1]
    plan_base = rows.bit_length() - 1 - (lax.axis_size("wide").bit_length() - 1) - 3
    merged = state.shape[-1] == rows * rows and plan_base >= 1 and gates.shape[0] >= 8
    return (merged_device if merged else general_device)(state, gates, *rest)


def solution(mesh):
    return jax.shard_map(
        on_device,
        mesh=mesh,
        in_specs=(
            P(None, "wide", "mid", "low", None),
            P(),
            P(),
            P(),
            P("wide", "mid", "low", None),
            P(),
            P(),
        ),
        out_specs=P(None, "wide", "mid", "low", None),
        check_vma=False,
    )
```

```python
from functools import partial

import jax
import jax.numpy as jnp
from jax import lax
from jax.experimental import pallas as pl
from jax.experimental.pallas import tpu as pltpu
from jax.sharding import PartitionSpec as P

HIGH = lax.Precision.HIGHEST
AXES = ("wide", "mid", "low")
VSPEC = pl.BlockSpec(memory_space=pltpu.VMEM)
HSPEC = pl.BlockSpec(memory_space=pltpu.HBM)
SSPEC = pl.BlockSpec(memory_space=pltpu.SMEM)


def split(value):
    high = value.astype(jnp.bfloat16)
    return high, (value - high.astype(jnp.float32)).astype(jnp.bfloat16)


def embed(value):
    half = value.shape[1] // 2
    return jnp.concatenate([value, jnp.concatenate([-value[:, half:], value[:, :half]], 1)], 0)


def dot(left, right, transposed=False):
    dims = (((1,), (1 if transposed else 0,)), ((), ()))
    return lax.dot_general(left, right, dims, preferred_element_type=jnp.float32)


def product(left, right, transposed=False):
    rows = left[0].shape[0]
    both = dot(jnp.concatenate(left, 0), right[0], transposed)
    return both[:rows] + both[rows:] + dot(left[0], right[1], transposed)


def complex_product(left, right):
    return product(left, tuple(embed(part) for part in right))


COSINE = (
    1.0,
    -0.5,
    0.0416666641831398,
    -0.0013888862449675798,
    2.480054899933748e-05,
    -2.753473324901279e-07,
    2.0603068140445657e-09,
    -9.720916779865085e-12,
)
SINE = (
    1.0,
    -0.1666666716337204,
    0.00833333283662796,
    -0.00019841254106722772,
    2.7556700388231548e-06,
    -2.5038662698761982e-08,
    1.5896317595576193e-10,
    -6.609633630347278e-13,
)


def series(square, terms):
    power = square
    terms = list(terms)
    while len(terms) > 1:
        terms = [terms[k] + terms[k + 1] * power for k in range(0, len(terms), 2)]
        power = power * power
    return terms[0]


def cosine_sine(angle):
    square = angle * angle
    return series(square, COSINE), angle * series(square, SINE)


def turn(value, angle):
    half = value.shape[1] // 2
    cosine, sine = cosine_sine(angle)
    real, imag = value[:, :half], value[:, half:]
    return jnp.concatenate([real * cosine - imag * sine, real * sine + imag * cosine], 1)


def side(ref, first=0):
    return jnp.concatenate([ref[first], ref[first + 1]], 1)


def gate(gates, number):
    return side(gates, 2 * number)


def scalars(ref):
    value = ref[...]
    return [value[0, place] for place in range(value.shape[1])]


class Plan:
    def __init__(self, rows, wide_count):
        self.rows = rows
        self.row_bits = rows.bit_length() - 1
        self.wide_bits = wide_count.bit_length() - 1
        self.low_base = self.row_bits - self.wide_bits - 3
        self.chunk = rows // (2 * wide_count)
        self.steps = [((wide, 0), (wide, 1)) for wide in range(wide_count - 1, 0, -1)]
        self.steps.insert(1, ((0, 1), (0, 1)))
        self.shared = [step for step in self.steps if step[0] != step[1]]


def by_core(step, core):
    return tuple(a if a == b else a ^ (core * (a ^ b)) for a, b in zip(*step))


def free_row(plan, inner, swap):
    base = plan.low_base
    lower = base + jnp.where(swap == 0, 1, 0)
    upper = base + jnp.where(swap == 2, 1, 2)
    return (
        (inner & ((1 << base) - 1))
        | jnp.left_shift(jnp.right_shift(inner, base) & 1, lower)
        | jnp.left_shift(jnp.right_shift(inner, base + 1) & 1, upper)
    )


def bits(value, place, count=1):
    return jnp.right_shift(value, place) & ((1 << count) - 1)


def sent_rows(plan, swaps, order):
    wide, core, low = lax.axis_index("wide"), lax.axis_index("mid") & 1, lax.axis_index("low") & 1
    targets = [(wide, low, core)]
    for step in plan.steps:
        wide_part, low_part = by_core(step, core)
        for to_core in (core, 1 - core)[: 2 if step in plan.shared else 1]:
            targets.append((wide ^ wide_part, low ^ low_part, to_core))
    base = plan.row_bits - 4
    position = plan.row_bits - 3 + swaps[0]
    places = [base + order[place] for place in range(4)]

    def reorder(row):
        old = row & ((1 << base) - 1)
        for place in range(4):
            old |= jnp.left_shift(bits(row, base + place), places[place])
        return old & ~jnp.left_shift(1, position), bits(old, position)

    inner = lax.broadcasted_iota(jnp.int32, (plan.chunk, plan.rows), 0)
    inner, inner_core = reorder(free_row(plan, inner, swaps[1]))
    result = []
    for to_wide, to_low, to_core in targets:
        outer = jnp.left_shift(to_low, plan.low_base + swaps[1])
        outer, outer_core = reorder(outer | (to_wide << (plan.row_bits - plan.wide_bits)))
        outer |= jnp.left_shift(to_core, position)
        result.append((inner | outer, inner_core | outer_core))
    return result


def received_rows(plan, swaps):
    wide, core, low = lax.axis_index("wide"), lax.axis_index("mid") & 1, lax.axis_index("low") & 1
    parts = [by_core(step, core) for step in plan.steps]
    parts += [by_core(step, 1 - core) for step in plan.shared]
    sources = [(wide, low)] + [(wide ^ part[0], low ^ part[1]) for part in parts]
    inner = lax.broadcasted_iota(jnp.int32, (plan.chunk, plan.rows), 0)
    inner = free_row(plan, inner, swaps[1])
    result = []
    for from_wide, from_low in sources:
        outer = jnp.left_shift(from_low, plan.low_base + swaps[1])
        result.append(inner | outer | (from_wide << (plan.row_bits - plan.wide_bits)))
    return result


def one_hot(plan, chunks):
    column = lax.broadcasted_iota(jnp.int32, (plan.chunk, plan.rows), 1)
    return jnp.concatenate([(column == rows).astype(jnp.bfloat16) for rows in chunks], 0)


def phase_kernel(plan, phase_top, factors):
    cosine, sine = cosine_sine(jnp.full(factors.shape, phase_top[0, 0, 0, 0]))
    first = lax.broadcasted_iota(jnp.int32, factors.shape, 0) == 0
    factors[...] = jnp.where(first, cosine, sine)


def spin(value, factors):
    half = value.shape[1] // 2
    cosine, sine = factors[:1], factors[1:2]
    real, imag = value[:, :half], value[:, half:]
    return jnp.concatenate([real * cosine - imag * sine, real * sine + imag * cosine], 1)


def front_kernel(plan, factors, state, gates, angle, swaps, order, own, high, low, *scratch):
    *buffers, sems = scratch
    sources = (swaps, order, gates.at[3], gates.at[1], angle, state)
    copies = [
        pltpu.make_async_copy(source, buffer, sems.at[place])
        for place, (source, buffer) in enumerate(zip(sources, buffers))
    ]
    for copy in copies:
        copy.start()
    swaps, order, gate_three, gate_one, angle, state = buffers
    copies[0].wait()
    copies[1].wait()
    chunks = sent_rows(plan, swaps, order)
    chosen = one_hot(plan, [rows for rows, _ in chunks])
    core = lax.axis_index("mid") & 1
    mask = jnp.concatenate([(held == core).astype(jnp.float32) for _, held in chunks], 0)
    mask = jnp.concatenate([mask, mask], 1)
    copies[2].wait()
    outer = tuple(dot(chosen, part).astype(jnp.bfloat16) for part in split(side(gate_three)))
    copies[3].wait()
    copies[4].wait()
    inner = turn(side(gate_one), angle[...])
    merged = complex_product(outer, split(inner))
    copies[5].wait()
    total = complex_product(split(merged * mask), split(side(state)))
    own[...] = spin(total, factors[...])
    high[...], low[...] = split(merged * (1.0 - mask))


def send_kernel(plan, own, high, low, state, factors, *sent):
    total = complex_product((high[...], low[...]), split(side(state)))
    total = own[...] + spin(total, factors[...])
    start = 0
    for ref in sent:
        ref[...] = total[start : start + ref.shape[0]]
        start += ref.shape[0]


def back_kernel(plan, count, gates, phase_low, swaps, kept, right_high, right_low, left_high, left_low):
    del kept
    rows = plan.rows

    def chain(numbers, value):
        for number in numbers:
            value = complex_product(split(gate(gates, number)), split(value))
        return value

    right = turn(gate(gates, 2), phase_low[...])
    right = complex_product(split(right), split(gate(gates, 0)))
    right = chain(range(4, count, 2), right)
    half = rows
    real, imag = right[:, :half], right[:, half:]
    right = jnp.concatenate(
        [jnp.concatenate([real, -imag], 1), jnp.concatenate([imag, real], 1)], 0
    )
    right_high[...], right_low[...] = split(right)
    placed = one_hot(plan, received_rows(plan, scalars(swaps)))
    first = tuple(
        jnp.concatenate([dot(part[:, :half], placed, True), dot(part[:, half:], placed, True)], 1)
        for part in split(gate(gates, 5))
    )
    left = complex_product(split(gate(gates, 7)), tuple(part.astype(jnp.bfloat16) for part in first))
    left = chain(range(9, count, 2), left)
    left_high[...], left_low[...] = split(left)


def sort_kernel(plan, *refs):
    give, place = refs[-1], 0
    for step, ref in zip(plan.steps, refs):
        if step in plan.shared:
            give[place : place + plan.chunk] = ref[plan.chunk :]
            place += plan.chunk


def kept_kernel(plan, *refs):
    *parts, right_high, right_low, high, low = refs
    value = jnp.concatenate([ref[: plan.chunk] for ref in parts], 0)
    value = product(split(value), (right_high[...], right_low[...]), True)
    high[...], low[...] = split(value)


def last_kernel(plan, high, low, given, right_high, right_low, left_high, left_low, out):
    value = split(product(split(given[...]), (right_high[...], right_low[...]), True))
    value = tuple(jnp.concatenate([a[...], b], 0) for a, b in zip((high, low), value))
    result = complex_product((left_high[...], left_low[...]), value)
    half = plan.rows
    out[0] = result[:, :half]
    out[1] = result[:, half:]


def call(kernel, shapes, args, specs, flops=0, scratch=()):
    args = [
        arg if spec is SSPEC else pltpu.with_memory_space_constraint(arg, spec.memory_space)
        for arg, spec in zip(args, specs)
    ]
    return pl.pallas_call(
        kernel,
        out_shape=[pltpu.VMEM(shape, dtype) for shape, dtype in shapes],
        in_specs=specs,
        out_specs=[VSPEC] * len(shapes),
        scratch_shapes=scratch,
        cost_estimate=pl.CostEstimate(flops=flops, bytes_accessed=1 << 17, transcendentals=0),
    )(*args)


def exchange(value, step=((0, 0), (0, 0)), flip=0):
    wides, mids, lows = (lax.axis_size(axis) for axis in AXES)
    pairs = []
    for wide in range(wides):
        for mid in range(mids):
            for low in range(lows):
                wide_part, low_part = step[mid & 1]
                to = ((wide ^ wide_part) * mids + (mid ^ flip)) * lows + (low ^ low_part)
                pairs.append(((wide * mids + mid) * lows + low, to))
    return lax.ppermute(value, AXES, pairs)


def merged_device(state, gates, phase_low, phase_mid, phase_top, swap_qubits, regroup_order):
    rows = gates.shape[-1]
    plan = Plan(rows, lax.axis_size("wide"))
    chunk = plan.chunk
    f32, bf16 = jnp.float32, jnp.bfloat16
    square = state.reshape(2, rows, rows)
    other = exchange(square, flip=1)
    (factors,) = call(partial(phase_kernel, plan), [((8, rows), f32)], (phase_top,), (SSPEC,))
    other_factors = exchange(factors, flip=1)
    pair = pltpu.VMEM((2, rows, rows), f32)
    scratch = [pltpu.SMEM(arg.shape, arg.dtype) for arg in (swap_qubits, regroup_order)]
    scratch += [pair, pair, pltpu.VMEM((1, rows), f32), pair, pltpu.SemaphoreType.DMA((6,))]
    own, high, low = call(
        partial(front_kernel, plan),
        [((rows, 2 * rows), f32), ((rows, 2 * rows), bf16), ((rows, 2 * rows), bf16)],
        (factors, square, gates, phase_mid.reshape(1, rows), swap_qubits, regroup_order),
        (VSPEC,) + (HSPEC,) * 5,
        scratch=scratch,
    )
    shapes = [(chunk, 2 * rows)]
    shapes += [(2 * chunk if step in plan.shared else chunk, 2 * rows) for step in plan.steps]
    local, *sent = call(
        partial(send_kernel, plan),
        [(shape, f32) for shape in shapes],
        (own, high, low, other, other_factors),
        (VSPEC,) * 5,
    )
    received = [exchange(value, step) for value, step in zip(sent, plan.steps)]
    wide_square = ((2 * rows, 2 * rows), bf16)
    tall = ((rows, 2 * rows), bf16)
    right_high, right_low, left_high, left_low = call(
        partial(back_kernel, plan, gates.shape[0]),
        [wide_square, wide_square, tall, tall],
        (
            gates.reshape(-1, rows, rows),
            phase_low.reshape(1, rows),
            swap_qubits.reshape(1, -1),
            local,
        ),
        (VSPEC,) * 4,
        flops=6 * 24 * rows**3,
    )
    (give,) = call(
        partial(sort_kernel, plan),
        [((len(plan.shared) * chunk, 2 * rows), f32)],
        (*received, left_low),
        (VSPEC,) * (len(received) + 1),
    )
    given = exchange(give, flip=1)
    kept_rows = (len(received) + 1) * chunk
    high, low = call(
        partial(kept_kernel, plan),
        [((kept_rows, 2 * rows), bf16)] * 2,
        (local, *received, right_high, right_low),
        (VSPEC,) * (len(received) + 3),
    )
    args = (high, low, given, right_high, right_low, left_high, left_low)
    out = pl.pallas_call(
        partial(last_kernel, plan),
        out_shape=jax.ShapeDtypeStruct((2, rows, rows), f32),
        in_specs=[VSPEC] * len(args),
    )(*[pltpu.with_memory_space_constraint(arg, pltpu.VMEM) for arg in args])
    return out.reshape(state.shape)


def partner(value, axis, stride):
    mask = 2**stride
    pairs = [(source, source ^ mask) for source in range(lax.axis_size(axis))]
    return lax.ppermute(value, axis, pairs)


def gate_inner(vector, real_gate, imag_gate):

    def product(values, matrix):
        return jnp.einsum("...b,ab->...a", values, matrix, precision=HIGH)

    real_part, imag_part = (vector[0], vector[1])
    return jnp.stack(
        [
            product(real_part, real_gate) - product(imag_part, imag_gate),
            product(real_part, imag_gate) + product(imag_part, real_gate),
        ]
    )


def gate_outer(vector, real_gate, imag_gate):

    def product(values, matrix):
        return jnp.einsum("ab,rbc->rac", matrix, values, precision=HIGH)

    real_part, imag_part = (vector[0], vector[1])
    return jnp.stack(
        [
            product(real_part, real_gate) - product(imag_part, imag_gate),
            product(real_part, imag_gate) + product(imag_part, real_gate),
        ]
    )


def apply_gate(vector, gates, number, gate_len):
    if number % 2 == 0:
        result = gate_inner(vector.reshape(2, -1, gate_len), gates[number, 0], gates[number, 1])
    else:
        result = gate_outer(
            vector.reshape(2, -1, gate_len, gate_len), gates[number, 0], gates[number, 1]
        )
    return result.reshape(2, -1)


def half_rows(vector, offset, base, own_bit, local_len):
    counter = jnp.arange(4, dtype=jnp.int32)
    lower = counter & jnp.left_shift(1, offset) - 1
    higher = jnp.right_shift(counter, offset)
    row_index = jnp.left_shift(higher, offset + 1) | jnp.left_shift(1 - own_bit, offset) | lower
    blocks = vector.reshape(2, local_len >> base + 3, 8, 1 << base)
    return (blocks, row_index, jnp.take(blocks, row_index, axis=2))


def move_bits(vector, lower, upper, local_len):
    if lower == upper:
        return vector
    shaped = vector.reshape(2, local_len >> upper + 1, 2, 1 << upper - lower - 1, 2, 1 << lower)
    return jnp.swapaxes(shaped, 2, 4).reshape(2, local_len)


def general_device(state, gates, phase_low, phase_mid, phase_top, swap_qubits, regroup_order):
    local_len = state.shape[-1]
    gate_len = gates.shape[-1]
    gate_count = gates.shape[0]
    local_bits = local_len.bit_length() - 1
    upper_len = local_len // (gate_len * gate_len)
    wide_count = lax.axis_size("wide")
    wide_bits = wide_count.bit_length() - 1
    vector = apply_gate(state.reshape(2, -1), gates, 0, gate_len)
    vector = vector.reshape(2, upper_len, gate_len, gate_len)
    angle = (
        phase_top.reshape(upper_len)[:, None, None]
        + phase_mid[None, :, None]
        + phase_low[None, None, :]
    )
    cosine = jnp.cos(angle)
    sine_part = jnp.sin(angle)
    vector = jnp.stack(
        [vector[0] * cosine - vector[1] * sine_part, vector[0] * sine_part + vector[1] * cosine]
    ).reshape(2, -1)
    for number in range(1, 4):
        vector = apply_gate(vector, gates, number, gate_len)
    mid_bit = lax.axis_index("mid") & 1
    blocks, row_index, sent_half = half_rows(
        vector, swap_qubits[0], local_bits - 3, mid_bit, local_len
    )
    received = partner(sent_half, "mid", 0)
    vector = blocks.at[:, :, row_index].set(received).reshape(2, local_len)
    row_ids = jnp.arange(16, dtype=jnp.int32)[:, None]
    row_bits = jnp.right_shift(row_ids, jnp.arange(4, dtype=jnp.int32)[None, :]) & 1
    order_index = jnp.sum(jnp.left_shift(row_bits, regroup_order[None, :]), axis=1)
    vector = jnp.take(vector.reshape(2, 16, local_len // 16), order_index, axis=1).reshape(
        2, local_len
    )
    low_base = local_bits - wide_bits - 3
    target = low_base + 2
    branches = [
        partial(move_bits, lower=low_base + place, upper=target, local_len=local_len)
        for place in range(3)
    ]
    vector = lax.switch(swap_qubits[1], branches, vector)
    shaped = vector.reshape(2, wide_count, 2, local_len // (2 * wide_count))
    moved = lax.all_to_all(
        lax.all_to_all(shaped, "wide", split_axis=1, concat_axis=1, tiled=True),
        "low",
        split_axis=2,
        concat_axis=2,
        tiled=True,
    )
    vector = lax.switch(swap_qubits[1], branches, moved.reshape(2, local_len))
    for number in range(4, gate_count):
        vector = apply_gate(vector, gates, number, gate_len)
    return vector.reshape(state.shape)


def on_device(state, gates, *rest):
    rows = gates.shape[-1]
    plan_base = rows.bit_length() - 1 - (lax.axis_size("wide").bit_length() - 1) - 3
    merged = state.shape[-1] == rows * rows and plan_base >= 1 and gates.shape[0] >= 8
    return (merged_device if merged else general_device)(state, gates, *rest)


def solution(mesh):
    return jax.shard_map(
        on_device,
        mesh=mesh,
        in_specs=(
            P(None, "wide", "mid", "low", None),
            P(),
            P(),
            P(),
            P("wide", "mid", "low", None),
            P(),
            P(),
        ),
        out_specs=P(None, "wide", "mid", "low", None),
        check_vma=False,
    )
```

```python
from functools import partial

import jax
import jax.numpy as jnp
from jax import lax
from jax.experimental import pallas as pl
from jax.experimental.pallas import tpu as pltpu
from jax.sharding import PartitionSpec as P

HIGH = lax.Precision.HIGHEST
BUSY = 1 << 29
LONG = 1 << 32
AXES = ("wide", "mid", "low")
VSPEC = pl.BlockSpec(memory_space=pltpu.VMEM)
SSPEC = pl.BlockSpec(memory_space=pltpu.SMEM)


def split(value):
    high = value.astype(jnp.bfloat16)
    return high, (value - high.astype(jnp.float32)).astype(jnp.bfloat16)


def embed(value):
    half = value.shape[1] // 2
    return jnp.concatenate([value, jnp.concatenate([-value[:, half:], value[:, :half]], 1)], 0)


def dot(left, right, transposed=False):
    dims = (((1,), (1 if transposed else 0,)), ((), ()))
    return lax.dot_general(left, right, dims, preferred_element_type=jnp.float32)


def product(left, right, transposed=False):
    rows = left[0].shape[0]
    both = dot(jnp.concatenate(left, 0), right[0], transposed)
    return both[:rows] + both[rows:] + dot(left[0], right[1], transposed)


def complex_product(left, right):
    return product(left, tuple(embed(part) for part in right))


COSINE = (
    1.0,
    -0.5,
    0.0416666641831398,
    -0.0013888862449675798,
    2.480054899933748e-05,
    -2.753473324901279e-07,
    2.0603068140445657e-09,
    -9.720916779865085e-12,
)
SINE = (
    1.0,
    -0.1666666716337204,
    0.00833333283662796,
    -0.00019841254106722772,
    2.7556700388231548e-06,
    -2.5038662698761982e-08,
    1.5896317595576193e-10,
    -6.609633630347278e-13,
)


def series(square, terms):
    power = square
    terms = list(terms)
    while len(terms) > 1:
        terms = [terms[k] + terms[k + 1] * power for k in range(0, len(terms), 2)]
        power = power * power
    return terms[0]


def cosine_sine(angle):
    square = angle * angle
    return series(square, COSINE), angle * series(square, SINE)


def turn(value, angle):
    half = value.shape[1] // 2
    cosine, sine = cosine_sine(angle)
    real, imag = value[:, :half], value[:, half:]
    return jnp.concatenate([real * cosine - imag * sine, real * sine + imag * cosine], 1)


def side(ref, first=0):
    return jnp.concatenate([ref[first], ref[first + 1]], 1)


def gate(gates, number):
    return side(gates, 2 * number)


def scalars(ref):
    value = ref[...]
    return [value[0, place] for place in range(value.shape[1])]


class Plan:
    def __init__(self, rows, wide_count):
        self.rows = rows
        self.row_bits = rows.bit_length() - 1
        self.wide_bits = wide_count.bit_length() - 1
        self.low_base = self.row_bits - self.wide_bits - 3
        self.chunk = rows // (2 * wide_count)
        self.steps = [((wide, 0), (wide, 1)) for wide in range(wide_count - 1, 0, -1)]
        self.steps.insert(1, ((0, 1), (0, 1)))
        self.shared = [step for step in self.steps if step[0] != step[1]]


def by_core(step, core):
    return tuple(a if a == b else a ^ (core * (a ^ b)) for a, b in zip(*step))


def free_row(plan, inner, swap):
    base = plan.low_base
    lower = base + jnp.where(swap == 0, 1, 0)
    upper = base + jnp.where(swap == 2, 1, 2)
    return (
        (inner & ((1 << base) - 1))
        | jnp.left_shift(jnp.right_shift(inner, base) & 1, lower)
        | jnp.left_shift(jnp.right_shift(inner, base + 1) & 1, upper)
    )


def bits(value, place, count=1):
    return jnp.right_shift(value, place) & ((1 << count) - 1)


def sent_rows(plan, swaps, order):
    wide, core, low = lax.axis_index("wide"), lax.axis_index("mid") & 1, lax.axis_index("low") & 1
    targets = [(wide, low, core)]
    for step in plan.steps:
        wide_part, low_part = by_core(step, core)
        for to_core in (core, 1 - core)[: 2 if step in plan.shared else 1]:
            targets.append((wide ^ wide_part, low ^ low_part, to_core))
    base = plan.row_bits - 4
    position = plan.row_bits - 3 + swaps[0]
    places = [base + order[place] for place in range(4)]

    def reorder(row):
        old = row & ((1 << base) - 1)
        for place in range(4):
            old |= jnp.left_shift(bits(row, base + place), places[place])
        return old & ~jnp.left_shift(1, position), bits(old, position)

    inner = lax.broadcasted_iota(jnp.int32, (plan.chunk, plan.rows), 0)
    inner, inner_core = reorder(free_row(plan, inner, swaps[1]))
    result = []
    for to_wide, to_low, to_core in targets:
        outer = jnp.left_shift(to_low, plan.low_base + swaps[1])
        outer, outer_core = reorder(outer | (to_wide << (plan.row_bits - plan.wide_bits)))
        outer |= jnp.left_shift(to_core, position)
        result.append((inner | outer, inner_core | outer_core))
    return result


def received_rows(plan, swaps):
    wide, core, low = lax.axis_index("wide"), lax.axis_index("mid") & 1, lax.axis_index("low") & 1
    parts = [by_core(step, core) for step in plan.steps]
    parts += [by_core(step, 1 - core) for step in plan.shared]
    sources = [(wide, low)] + [(wide ^ part[0], low ^ part[1]) for part in parts]
    inner = lax.broadcasted_iota(jnp.int32, (plan.chunk, plan.rows), 0)
    inner = free_row(plan, inner, swaps[1])
    result = []
    for from_wide, from_low in sources:
        outer = jnp.left_shift(from_low, plan.low_base + swaps[1])
        result.append(inner | outer | (from_wide << (plan.row_bits - plan.wide_bits)))
    return result


def one_hot(plan, chunks):
    column = lax.broadcasted_iota(jnp.int32, (plan.chunk, plan.rows), 1)
    return jnp.concatenate([(column == rows).astype(jnp.bfloat16) for rows in chunks], 0)


def phase_kernel(plan, phase_top, factors):
    cosine, sine = cosine_sine(jnp.full(factors.shape, phase_top[0, 0, 0, 0]))
    first = lax.broadcasted_iota(jnp.int32, factors.shape, 0) == 0
    factors[...] = jnp.where(first, cosine, sine)


def spin(value, factors):
    half = value.shape[1] // 2
    cosine, sine = factors[:1], factors[1:2]
    real, imag = value[:, :half], value[:, half:]
    return jnp.concatenate([real * cosine - imag * sine, real * sine + imag * cosine], 1)


def front_kernel(plan, state, factors, gates, angle, swaps, order, own, high, low):
    chunks = sent_rows(plan, scalars(swaps), scalars(order))
    chosen = one_hot(plan, [rows for rows, _ in chunks])
    core = lax.axis_index("mid") & 1
    mask = jnp.concatenate([(held == core).astype(jnp.float32) for _, held in chunks], 0)
    mask = jnp.concatenate([mask, mask], 1)
    outer = tuple(dot(chosen, part).astype(jnp.bfloat16) for part in split(gate(gates, 3)))
    inner = turn(gate(gates, 1), angle[...])
    merged = complex_product(outer, split(inner))
    own[...] = spin(complex_product(split(merged * mask), split(side(state))), factors[...])
    high[...], low[...] = split(merged * (1.0 - mask))


def send_kernel(plan, own, high, low, state, factors, *sent):
    total = complex_product((high[...], low[...]), split(side(state)))
    total = own[...] + spin(total, factors[...])
    start = 0
    for ref in sent:
        ref[...] = total[start : start + ref.shape[0]]
        start += ref.shape[0]


def chain(factors):
    while len(factors) > 1:
        pairs = [factors[k : k + 2] for k in range(0, len(factors), 2)]
        factors = [
            complex_product(split(pair[0]), split(pair[1])) if len(pair) == 2 else pair[0]
            for pair in pairs
        ]
    return factors[0]


def right_kernel(plan, count, gates, phase_low, high, low):
    factors = [gate(gates, number) for number in range((count - 1) // 2 * 2, 2, -2)]
    value = chain(factors + [turn(gate(gates, 2), phase_low[...]), gate(gates, 0)])
    real, imag = value[:, : plan.rows], value[:, plan.rows :]
    high[...], low[...] = split(
        jnp.concatenate(
            [jnp.concatenate([real, -imag], 1), jnp.concatenate([imag, real], 1)], 0
        )
    )


def left_kernel(plan, count, gates, swaps, high, low):
    placed = one_hot(plan, received_rows(plan, scalars(swaps)))
    first = gate(gates, 5)
    first = [
        sum(dot(part, placed, True) for part in split(half))
        for half in (first[:, : plan.rows], first[:, plan.rows :])
    ]
    factors = [gate(gates, number) for number in range((count - 2) // 2 * 2 + 1, 5, -2)]
    high[...], low[...] = split(chain(factors + [jnp.concatenate(first, 1)]))


def back_kernel(plan, count, gates, phase_low, swaps, kept, *factors):
    del kept
    right_kernel(plan, count, gates, phase_low, *factors[:2])
    left_kernel(plan, count, gates, swaps, *factors[2:])


def sort_kernel(plan, *refs):
    give = refs[-1]
    for place, ref in enumerate(refs[: len(plan.shared)]):
        give[place * plan.chunk : (place + 1) * plan.chunk] = ref[plan.chunk :]


def kept_kernel(plan, *refs):
    *parts, right_high, right_low, high, low = refs
    value = jnp.concatenate([ref[: plan.chunk] for ref in parts], 0)
    value = product(split(value), (right_high[...], right_low[...]), True)
    high[...], low[...] = split(value)


def last_kernel(plan, high, low, given, right_high, right_low, left_high, left_low, out):
    value = split(product(split(given[...]), (right_high[...], right_low[...]), True))
    value = tuple(jnp.concatenate([a[...], b], 0) for a, b in zip((high, low), value))
    result = complex_product((left_high[...], left_low[...]), value)
    half = plan.rows
    out[0] = result[:, :half]
    out[1] = result[:, half:]


def call(kernel, shapes, args, specs, flops=0):
    args = [
        arg if spec is SSPEC else pltpu.with_memory_space_constraint(arg, spec.memory_space)
        for arg, spec in zip(args, specs)
    ]
    return pl.pallas_call(
        kernel,
        out_shape=[pltpu.VMEM(shape, dtype) for shape, dtype in shapes],
        in_specs=specs,
        out_specs=[VSPEC] * len(shapes),
        cost_estimate=pl.CostEstimate(flops=flops, bytes_accessed=1 << 17, transcendentals=0),
    )(*args)


def exchange(value, step=((0, 0), (0, 0)), flip=0):
    wides, mids, lows = (lax.axis_size(axis) for axis in AXES)
    pairs = []
    for wide in range(wides):
        for mid in range(mids):
            for low in range(lows):
                wide_part, low_part = step[mid & 1]
                to = ((wide ^ wide_part) * mids + (mid ^ flip)) * lows + (low ^ low_part)
                pairs.append(((wide * mids + mid) * lows + low, to))
    return lax.ppermute(value, AXES, pairs)


def merged_device(state, gates, phase_low, phase_mid, phase_top, swap_qubits, regroup_order):
    rows = gates.shape[-1]
    plan = Plan(rows, lax.axis_size("wide"))
    chunk = plan.chunk
    f32, bf16 = jnp.float32, jnp.bfloat16
    gates = gates.reshape(-1, rows, rows)
    swaps, order = swap_qubits.reshape(1, -1), regroup_order.reshape(1, -1)
    square = state.reshape(2, rows, rows)
    other = exchange(square, flip=1)
    (factors,) = call(partial(phase_kernel, plan), [((8, rows), f32)], (phase_top,), (SSPEC,), BUSY)
    other_factors = exchange(factors, flip=1)
    own, high, low = call(
        partial(front_kernel, plan),
        [((rows, 2 * rows), f32), ((rows, 2 * rows), bf16), ((rows, 2 * rows), bf16)],
        (square, factors, gates, phase_mid.reshape(1, rows), swaps, order),
        (VSPEC,) * 6,
    )
    shapes = [(chunk, 2 * rows)]
    shapes += [(2 * chunk if step in plan.shared else chunk, 2 * rows) for step in plan.steps]
    local, *sent = call(
        partial(send_kernel, plan),
        [(shape, f32) for shape in shapes],
        (own, high, low, other, other_factors),
        (VSPEC,) * 5,
    )
    received = [exchange(value, step) for value, step in zip(sent, plan.steps)]
    right_high, right_low, left_high, left_low = call(
        partial(back_kernel, plan, gates.shape[0] // 2),
        [((2 * rows, 2 * rows), bf16)] * 2 + [((rows, 2 * rows), bf16)] * 2,
        (gates, phase_low.reshape(1, rows), swaps, local),
        (VSPEC,) * 4,
    )
    shared = [value for value, step in zip(received, plan.steps) if step in plan.shared]
    (give,) = call(
        partial(sort_kernel, plan),
        [((len(plan.shared) * chunk, 2 * rows), f32)],
        (*shared, left_low),
        (VSPEC,) * (len(shared) + 1),
    )
    given = exchange(give, flip=1)
    kept_rows = (len(received) + 1) * chunk
    high, low = call(
        partial(kept_kernel, plan),
        [((kept_rows, 2 * rows), bf16)] * 2,
        (local, *received, right_high, right_low),
        (VSPEC,) * (len(received) + 3),
        LONG,
    )
    args = (high, low, given, right_high, right_low, left_high, left_low)
    out = pl.pallas_call(
        partial(last_kernel, plan),
        out_shape=jax.ShapeDtypeStruct((2, rows, rows), f32),
        in_specs=[VSPEC] * len(args),
    )(*[pltpu.with_memory_space_constraint(arg, pltpu.VMEM) for arg in args])
    return out.reshape(state.shape)


def partner(value, axis, stride):
    mask = 2**stride
    pairs = [(source, source ^ mask) for source in range(lax.axis_size(axis))]
    return lax.ppermute(value, axis, pairs)


def gate_inner(vector, real_gate, imag_gate):

    def product(values, matrix):
        return jnp.einsum("...b,ab->...a", values, matrix, precision=HIGH)

    real_part, imag_part = (vector[0], vector[1])
    return jnp.stack(
        [
            product(real_part, real_gate) - product(imag_part, imag_gate),
            product(real_part, imag_gate) + product(imag_part, real_gate),
        ]
    )


def gate_outer(vector, real_gate, imag_gate):

    def product(values, matrix):
        return jnp.einsum("ab,rbc->rac", matrix, values, precision=HIGH)

    real_part, imag_part = (vector[0], vector[1])
    return jnp.stack(
        [
            product(real_part, real_gate) - product(imag_part, imag_gate),
            product(real_part, imag_gate) + product(imag_part, real_gate),
        ]
    )


def apply_gate(vector, gates, number, gate_len):
    if number % 2 == 0:
        result = gate_inner(vector.reshape(2, -1, gate_len), gates[number, 0], gates[number, 1])
    else:
        result = gate_outer(
            vector.reshape(2, -1, gate_len, gate_len), gates[number, 0], gates[number, 1]
        )
    return result.reshape(2, -1)


def half_rows(vector, offset, base, own_bit, local_len):
    counter = jnp.arange(4, dtype=jnp.int32)
    lower = counter & jnp.left_shift(1, offset) - 1
    higher = jnp.right_shift(counter, offset)
    row_index = jnp.left_shift(higher, offset + 1) | jnp.left_shift(1 - own_bit, offset) | lower
    blocks = vector.reshape(2, local_len >> base + 3, 8, 1 << base)
    return (blocks, row_index, jnp.take(blocks, row_index, axis=2))


def move_bits(vector, lower, upper, local_len):
    if lower == upper:
        return vector
    shaped = vector.reshape(2, local_len >> upper + 1, 2, 1 << upper - lower - 1, 2, 1 << lower)
    return jnp.swapaxes(shaped, 2, 4).reshape(2, local_len)


def general_device(state, gates, phase_low, phase_mid, phase_top, swap_qubits, regroup_order):
    local_len = state.shape[-1]
    gate_len = gates.shape[-1]
    gate_count = gates.shape[0]
    local_bits = local_len.bit_length() - 1
    upper_len = local_len // (gate_len * gate_len)
    wide_count = lax.axis_size("wide")
    wide_bits = wide_count.bit_length() - 1
    vector = apply_gate(state.reshape(2, -1), gates, 0, gate_len)
    vector = vector.reshape(2, upper_len, gate_len, gate_len)
    angle = (
        phase_top.reshape(upper_len)[:, None, None]
        + phase_mid[None, :, None]
        + phase_low[None, None, :]
    )
    cosine = jnp.cos(angle)
    sine_part = jnp.sin(angle)
    vector = jnp.stack(
        [vector[0] * cosine - vector[1] * sine_part, vector[0] * sine_part + vector[1] * cosine]
    ).reshape(2, -1)
    for number in range(1, 4):
        vector = apply_gate(vector, gates, number, gate_len)
    mid_bit = lax.axis_index("mid") & 1
    blocks, row_index, sent_half = half_rows(
        vector, swap_qubits[0], local_bits - 3, mid_bit, local_len
    )
    received = partner(sent_half, "mid", 0)
    vector = blocks.at[:, :, row_index].set(received).reshape(2, local_len)
    row_ids = jnp.arange(16, dtype=jnp.int32)[:, None]
    row_bits = jnp.right_shift(row_ids, jnp.arange(4, dtype=jnp.int32)[None, :]) & 1
    order_index = jnp.sum(jnp.left_shift(row_bits, regroup_order[None, :]), axis=1)
    vector = jnp.take(vector.reshape(2, 16, local_len // 16), order_index, axis=1).reshape(
        2, local_len
    )
    low_base = local_bits - wide_bits - 3
    target = low_base + 2
    branches = [
        partial(move_bits, lower=low_base + place, upper=target, local_len=local_len)
        for place in range(3)
    ]
    vector = lax.switch(swap_qubits[1], branches, vector)
    shaped = vector.reshape(2, wide_count, 2, local_len // (2 * wide_count))
    moved = lax.all_to_all(
        lax.all_to_all(shaped, "wide", split_axis=1, concat_axis=1, tiled=True),
        "low",
        split_axis=2,
        concat_axis=2,
        tiled=True,
    )
    vector = lax.switch(swap_qubits[1], branches, moved.reshape(2, local_len))
    for number in range(4, gate_count):
        vector = apply_gate(vector, gates, number, gate_len)
    return vector.reshape(state.shape)


def on_device(state, gates, *rest):
    rows = gates.shape[-1]
    plan_base = rows.bit_length() - 1 - (lax.axis_size("wide").bit_length() - 1) - 3
    merged = state.shape[-1] == rows * rows and plan_base >= 1 and gates.shape[0] >= 8
    return (merged_device if merged else general_device)(state, gates, *rest)


def solution(mesh):
    return jax.shard_map(
        on_device,
        mesh=mesh,
        in_specs=(
            P(None, "wide", "mid", "low", None),
            P(),
            P(),
            P(),
            P("wide", "mid", "low", None),
            P(),
            P(),
        ),
        out_specs=P(None, "wide", "mid", "low", None),
        check_vma=False,
    )
```

```python
from functools import partial

import jax
import jax.numpy as jnp
from jax import lax
from jax.experimental import pallas as pl
from jax.experimental.pallas import tpu as pltpu
from jax.sharding import PartitionSpec as P

HIGH = lax.Precision.HIGHEST
BUSY = 1 << 29
LONG = 1 << 32
AXES = ("wide", "mid", "low")
VSPEC = pl.BlockSpec(memory_space=pltpu.VMEM)
SSPEC = pl.BlockSpec(memory_space=pltpu.SMEM)


def split(value):
    high = value.astype(jnp.bfloat16)
    return high, (value - high.astype(jnp.float32)).astype(jnp.bfloat16)


def embed(value):
    half = value.shape[1] // 2
    return jnp.concatenate([value, jnp.concatenate([-value[:, half:], value[:, :half]], 1)], 0)


def dot(left, right, transposed=False):
    dims = (((1,), (1 if transposed else 0,)), ((), ()))
    return lax.dot_general(left, right, dims, preferred_element_type=jnp.float32)


def product(left, right, transposed=False):
    rows = left[0].shape[0]
    both = dot(jnp.concatenate(left, 0), right[0], transposed)
    return both[:rows] + both[rows:] + dot(left[0], right[1], transposed)


def complex_product(left, right):
    return product(left, tuple(embed(part) for part in right))


COSINE = (
    1.0,
    -0.5,
    0.0416666641831398,
    -0.0013888862449675798,
    2.480054899933748e-05,
    -2.753473324901279e-07,
    2.0603068140445657e-09,
    -9.720916779865085e-12,
)
SINE = (
    1.0,
    -0.1666666716337204,
    0.00833333283662796,
    -0.00019841254106722772,
    2.7556700388231548e-06,
    -2.5038662698761982e-08,
    1.5896317595576193e-10,
    -6.609633630347278e-13,
)


def series(square, terms):
    power = square
    terms = list(terms)
    while len(terms) > 1:
        terms = [terms[k] + terms[k + 1] * power for k in range(0, len(terms), 2)]
        power = power * power
    return terms[0]


def cosine_sine(angle):
    square = angle * angle
    return series(square, COSINE), angle * series(square, SINE)


def turn(value, angle):
    half = value.shape[1] // 2
    cosine, sine = cosine_sine(angle)
    real, imag = value[:, :half], value[:, half:]
    return jnp.concatenate([real * cosine - imag * sine, real * sine + imag * cosine], 1)


def side(ref, first=0):
    return jnp.concatenate([ref[first], ref[first + 1]], 1)


def gate(gates, number):
    return side(gates, 2 * number)


def scalars(ref):
    value = ref[...]
    return [value[0, place] for place in range(value.shape[1])]


class Plan:
    def __init__(self, rows, wide_count):
        self.rows = rows
        self.row_bits = rows.bit_length() - 1
        self.wide_bits = wide_count.bit_length() - 1
        self.low_base = self.row_bits - self.wide_bits - 3
        self.chunk = rows // (2 * wide_count)
        half = wide_count // 2
        tops = [tuple(range(k, min(k + 2, wide_count))) for k in range(half, wide_count, 2)]
        self.steps = [((pair[0], pair[-1]), (0, 1)) for pair in tops]
        self.steps += [((pair[1], pair[0]), (0, 1)) for pair in tops if len(pair) == 2]
        near = range(half - 1, 0, -1)
        self.steps += [((offset, offset), (1, 1)) for offset in near]
        self.steps.append(((0, 0), (1, 1)))
        self.steps += [((offset, offset), (0, 0)) for offset in near]
        self.shared = [step for step in self.steps if step[1][0] != step[1][1]]


def choose(flag, pair):
    return pair[0] if pair[0] == pair[1] else pair[0] ^ (flag * (pair[0] ^ pair[1]))


def free_row(plan, inner, swap):
    base = plan.low_base
    lower = base + jnp.where(swap == 0, 1, 0)
    upper = base + jnp.where(swap == 2, 1, 2)
    return (
        (inner & ((1 << base) - 1))
        | jnp.left_shift(jnp.right_shift(inner, base) & 1, lower)
        | jnp.left_shift(jnp.right_shift(inner, base + 1) & 1, upper)
    )


def bits(value, place, count=1):
    return jnp.right_shift(value, place) & ((1 << count) - 1)


def sent_rows(plan, swaps, order):
    wide, core, low = lax.axis_index("wide"), lax.axis_index("mid") & 1, lax.axis_index("low") & 1
    targets = [(wide, low, core)]
    half = wide >> (plan.wide_bits - 1)
    for step in plan.steps:
        to_wide, to_low = wide ^ choose(half, step[0]), low ^ choose(core, step[1])
        for to_core in (core, 1 - core)[: 2 if step in plan.shared else 1]:
            targets.append((to_wide, to_low, to_core))
    base = plan.row_bits - 4
    position = plan.row_bits - 3 + swaps[0]
    places = [base + order[place] for place in range(4)]

    def reorder(row):
        old = row & ((1 << base) - 1)
        for place in range(4):
            old |= jnp.left_shift(bits(row, base + place), places[place])
        return old & ~jnp.left_shift(1, position), bits(old, position)

    inner = lax.broadcasted_iota(jnp.int32, (plan.chunk, plan.rows), 0)
    inner, inner_core = reorder(free_row(plan, inner, swaps[1]))
    result = []
    for to_wide, to_low, to_core in targets:
        outer = jnp.left_shift(to_low, plan.low_base + swaps[1])
        outer, outer_core = reorder(outer | (to_wide << (plan.row_bits - plan.wide_bits)))
        outer |= jnp.left_shift(to_core, position)
        result.append((inner | outer, inner_core | outer_core))
    return result


def received_rows(plan, swaps):
    wide, core, low = lax.axis_index("wide"), lax.axis_index("mid") & 1, lax.axis_index("low") & 1
    half = wide >> (plan.wide_bits - 1)
    sources = [(wide, low)]
    for server, steps in ((core, plan.steps), (1 - core, plan.shared)):
        for step in steps:
            sources.append((wide ^ choose(1 - half, step[0]), low ^ choose(server, step[1])))
    inner = lax.broadcasted_iota(jnp.int32, (plan.chunk, plan.rows), 0)
    inner = free_row(plan, inner, swaps[1])
    result = []
    for from_wide, from_low in sources:
        outer = jnp.left_shift(from_low, plan.low_base + swaps[1])
        result.append(inner | outer | (from_wide << (plan.row_bits - plan.wide_bits)))
    return result


def one_hot(plan, chunks):
    column = lax.broadcasted_iota(jnp.int32, (plan.chunk, plan.rows), 1)
    return jnp.concatenate([(column == rows).astype(jnp.bfloat16) for rows in chunks], 0)


def phase_kernel(plan, phase_top, factors):
    cosine, sine = cosine_sine(jnp.full(factors.shape, phase_top[0, 0, 0, 0]))
    first = lax.broadcasted_iota(jnp.int32, factors.shape, 0) == 0
    factors[...] = jnp.where(first, cosine, sine)


def spin(value, factors):
    half = value.shape[1] // 2
    cosine, sine = factors[:1], factors[1:2]
    real, imag = value[:, :half], value[:, half:]
    return jnp.concatenate([real * cosine - imag * sine, real * sine + imag * cosine], 1)


def front_kernel(plan, state, factors, gates, angle, swaps, order, own, high, low):
    chunks = sent_rows(plan, scalars(swaps), scalars(order))
    chosen = one_hot(plan, [rows for rows, _ in chunks])
    core = lax.axis_index("mid") & 1
    mask = jnp.concatenate([(held == core).astype(jnp.float32) for _, held in chunks], 0)
    mask = jnp.concatenate([mask, mask], 1)
    outer = tuple(dot(chosen, part).astype(jnp.bfloat16) for part in split(gate(gates, 3)))
    inner = turn(gate(gates, 1), angle[...])
    merged = complex_product(outer, split(inner))
    own[...] = spin(complex_product(split(merged * mask), split(side(state))), factors[...])
    high[...], low[...] = split(merged * (1.0 - mask))


def send_kernel(plan, own, high, low, state, factors, *sent):
    total = complex_product((high[...], low[...]), split(side(state)))
    total = own[...] + spin(total, factors[...])
    start = 0
    for ref in sent:
        ref[...] = total[start : start + ref.shape[0]]
        start += ref.shape[0]


def chain(factors):
    while len(factors) > 1:
        pairs = [factors[k : k + 2] for k in range(0, len(factors), 2)]
        factors = [
            complex_product(split(pair[0]), split(pair[1])) if len(pair) == 2 else pair[0]
            for pair in pairs
        ]
    return factors[0]


def right_kernel(plan, count, gates, phase_low, high, low):
    factors = [gate(gates, number) for number in range((count - 1) // 2 * 2, 2, -2)]
    value = chain(factors + [turn(gate(gates, 2), phase_low[...]), gate(gates, 0)])
    real, imag = value[:, : plan.rows], value[:, plan.rows :]
    high[...], low[...] = split(
        jnp.concatenate(
            [jnp.concatenate([real, -imag], 1), jnp.concatenate([imag, real], 1)], 0
        )
    )


def left_kernel(plan, count, gates, swaps, high, low):
    placed = one_hot(plan, received_rows(plan, scalars(swaps)))
    first = gate(gates, 5)
    first = [
        sum(dot(part, placed, True) for part in split(half))
        for half in (first[:, : plan.rows], first[:, plan.rows :])
    ]
    factors = [gate(gates, number) for number in range((count - 2) // 2 * 2 + 1, 5, -2)]
    high[...], low[...] = split(chain(factors + [jnp.concatenate(first, 1)]))


def back_kernel(plan, count, gates, phase_low, swaps, kept, *factors):
    del kept
    right_kernel(plan, count, gates, phase_low, *factors[:2])
    left_kernel(plan, count, gates, swaps, *factors[2:])


def sort_kernel(plan, *refs):
    give = refs[-1]
    for place, ref in enumerate(refs[: len(plan.shared)]):
        give[place * plan.chunk : (place + 1) * plan.chunk] = ref[plan.chunk :]


def kept_kernel(plan, *refs):
    *parts, right_high, right_low, high, low = refs
    value = jnp.concatenate([ref[: plan.chunk] for ref in parts], 0)
    value = product(split(value), (right_high[...], right_low[...]), True)
    high[...], low[...] = split(value)


def last_kernel(plan, high, low, given, right_high, right_low, left_high, left_low, out):
    value = split(product(split(given[...]), (right_high[...], right_low[...]), True))
    value = tuple(jnp.concatenate([a[...], b], 0) for a, b in zip((high, low), value))
    result = complex_product((left_high[...], left_low[...]), value)
    half = plan.rows
    out[0] = result[:, :half]
    out[1] = result[:, half:]


def call(kernel, shapes, args, specs, flops=0):
    args = [
        arg if spec is SSPEC else pltpu.with_memory_space_constraint(arg, spec.memory_space)
        for arg, spec in zip(args, specs)
    ]
    return pl.pallas_call(
        kernel,
        out_shape=[pltpu.VMEM(shape, dtype) for shape, dtype in shapes],
        in_specs=specs,
        out_specs=[VSPEC] * len(shapes),
        cost_estimate=pl.CostEstimate(flops=flops, bytes_accessed=1 << 17, transcendentals=0),
    )(*args)


def exchange(value, step=((0, 0), (0, 0)), flip=0):
    wides, mids, lows = (lax.axis_size(axis) for axis in AXES)
    pairs = []
    for wide in range(wides):
        for mid in range(mids):
            for low in range(lows):
                to_wide = wide ^ step[0][2 * wide // wides]
                to = (to_wide * mids + (mid ^ flip)) * lows + (low ^ step[1][mid & 1])
                pairs.append(((wide * mids + mid) * lows + low, to))
    return lax.ppermute(value, AXES, pairs)


def merged_device(state, gates, phase_low, phase_mid, phase_top, swap_qubits, regroup_order):
    rows = gates.shape[-1]
    plan = Plan(rows, lax.axis_size("wide"))
    chunk = plan.chunk
    f32, bf16 = jnp.float32, jnp.bfloat16
    gates = gates.reshape(-1, rows, rows)
    swaps, order = swap_qubits.reshape(1, -1), regroup_order.reshape(1, -1)
    square = state.reshape(2, rows, rows)
    other = exchange(square, flip=1)
    (factors,) = call(partial(phase_kernel, plan), [((8, rows), f32)], (phase_top,), (SSPEC,), BUSY)
    other_factors = exchange(factors, flip=1)
    own, high, low = call(
        partial(front_kernel, plan),
        [((rows, 2 * rows), f32), ((rows, 2 * rows), bf16), ((rows, 2 * rows), bf16)],
        (square, factors, gates, phase_mid.reshape(1, rows), swaps, order),
        (VSPEC,) * 6,
    )
    shapes = [(chunk, 2 * rows)]
    shapes += [(2 * chunk if step in plan.shared else chunk, 2 * rows) for step in plan.steps]
    local, *sent = call(
        partial(send_kernel, plan),
        [(shape, f32) for shape in shapes],
        (own, high, low, other, other_factors),
        (VSPEC,) * 5,
    )
    received = [exchange(value, step) for value, step in zip(sent, plan.steps)]
    right_high, right_low, left_high, left_low = call(
        partial(back_kernel, plan, gates.shape[0] // 2),
        [((2 * rows, 2 * rows), bf16)] * 2 + [((rows, 2 * rows), bf16)] * 2,
        (gates, phase_low.reshape(1, rows), swaps, local),
        (VSPEC,) * 4,
    )
    shared = [value for value, step in zip(received, plan.steps) if step in plan.shared]
    (give,) = call(
        partial(sort_kernel, plan),
        [((len(plan.shared) * chunk, 2 * rows), f32)],
        (*shared, left_low),
        (VSPEC,) * (len(shared) + 1),
    )
    given = exchange(give, flip=1)
    kept_rows = (len(received) + 1) * chunk
    high, low = call(
        partial(kept_kernel, plan),
        [((kept_rows, 2 * rows), bf16)] * 2,
        (local, *received, right_high, right_low),
        (VSPEC,) * (len(received) + 3),
        LONG,
    )
    args = (high, low, given, right_high, right_low, left_high, left_low)
    out = pl.pallas_call(
        partial(last_kernel, plan),
        out_shape=jax.ShapeDtypeStruct((2, rows, rows), f32),
        in_specs=[VSPEC] * len(args),
    )(*[pltpu.with_memory_space_constraint(arg, pltpu.VMEM) for arg in args])
    return out.reshape(state.shape)


def partner(value, axis, stride):
    mask = 2**stride
    pairs = [(source, source ^ mask) for source in range(lax.axis_size(axis))]
    return lax.ppermute(value, axis, pairs)


def gate_inner(vector, real_gate, imag_gate):

    def product(values, matrix):
        return jnp.einsum("...b,ab->...a", values, matrix, precision=HIGH)

    real_part, imag_part = (vector[0], vector[1])
    return jnp.stack(
        [
            product(real_part, real_gate) - product(imag_part, imag_gate),
            product(real_part, imag_gate) + product(imag_part, real_gate),
        ]
    )


def gate_outer(vector, real_gate, imag_gate):

    def product(values, matrix):
        return jnp.einsum("ab,rbc->rac", matrix, values, precision=HIGH)

    real_part, imag_part = (vector[0], vector[1])
    return jnp.stack(
        [
            product(real_part, real_gate) - product(imag_part, imag_gate),
            product(real_part, imag_gate) + product(imag_part, real_gate),
        ]
    )


def apply_gate(vector, gates, number, gate_len):
    if number % 2 == 0:
        result = gate_inner(vector.reshape(2, -1, gate_len), gates[number, 0], gates[number, 1])
    else:
        result = gate_outer(
            vector.reshape(2, -1, gate_len, gate_len), gates[number, 0], gates[number, 1]
        )
    return result.reshape(2, -1)


def half_rows(vector, offset, base, own_bit, local_len):
    counter = jnp.arange(4, dtype=jnp.int32)
    lower = counter & jnp.left_shift(1, offset) - 1
    higher = jnp.right_shift(counter, offset)
    row_index = jnp.left_shift(higher, offset + 1) | jnp.left_shift(1 - own_bit, offset) | lower
    blocks = vector.reshape(2, local_len >> base + 3, 8, 1 << base)
    return (blocks, row_index, jnp.take(blocks, row_index, axis=2))


def move_bits(vector, lower, upper, local_len):
    if lower == upper:
        return vector
    shaped = vector.reshape(2, local_len >> upper + 1, 2, 1 << upper - lower - 1, 2, 1 << lower)
    return jnp.swapaxes(shaped, 2, 4).reshape(2, local_len)


def general_device(state, gates, phase_low, phase_mid, phase_top, swap_qubits, regroup_order):
    local_len = state.shape[-1]
    gate_len = gates.shape[-1]
    gate_count = gates.shape[0]
    local_bits = local_len.bit_length() - 1
    upper_len = local_len // (gate_len * gate_len)
    wide_count = lax.axis_size("wide")
    wide_bits = wide_count.bit_length() - 1
    vector = apply_gate(state.reshape(2, -1), gates, 0, gate_len)
    vector = vector.reshape(2, upper_len, gate_len, gate_len)
    angle = (
        phase_top.reshape(upper_len)[:, None, None]
        + phase_mid[None, :, None]
        + phase_low[None, None, :]
    )
    cosine = jnp.cos(angle)
    sine_part = jnp.sin(angle)
    vector = jnp.stack(
        [vector[0] * cosine - vector[1] * sine_part, vector[0] * sine_part + vector[1] * cosine]
    ).reshape(2, -1)
    for number in range(1, 4):
        vector = apply_gate(vector, gates, number, gate_len)
    mid_bit = lax.axis_index("mid") & 1
    blocks, row_index, sent_half = half_rows(
        vector, swap_qubits[0], local_bits - 3, mid_bit, local_len
    )
    received = partner(sent_half, "mid", 0)
    vector = blocks.at[:, :, row_index].set(received).reshape(2, local_len)
    row_ids = jnp.arange(16, dtype=jnp.int32)[:, None]
    row_bits = jnp.right_shift(row_ids, jnp.arange(4, dtype=jnp.int32)[None, :]) & 1
    order_index = jnp.sum(jnp.left_shift(row_bits, regroup_order[None, :]), axis=1)
    vector = jnp.take(vector.reshape(2, 16, local_len // 16), order_index, axis=1).reshape(
        2, local_len
    )
    low_base = local_bits - wide_bits - 3
    target = low_base + 2
    branches = [
        partial(move_bits, lower=low_base + place, upper=target, local_len=local_len)
        for place in range(3)
    ]
    vector = lax.switch(swap_qubits[1], branches, vector)
    shaped = vector.reshape(2, wide_count, 2, local_len // (2 * wide_count))
    moved = lax.all_to_all(
        lax.all_to_all(shaped, "wide", split_axis=1, concat_axis=1, tiled=True),
        "low",
        split_axis=2,
        concat_axis=2,
        tiled=True,
    )
    vector = lax.switch(swap_qubits[1], branches, moved.reshape(2, local_len))
    for number in range(4, gate_count):
        vector = apply_gate(vector, gates, number, gate_len)
    return vector.reshape(state.shape)


def on_device(state, gates, *rest):
    rows = gates.shape[-1]
    sizes = [lax.axis_size(axis) for axis in AXES]
    base = rows.bit_length() - sizes[0].bit_length() - 3
    merged = state.shape[-1] == rows * rows and base >= 2 and min(sizes) >= 2
    return (merged_device if merged else general_device)(state, gates, *rest)


def solution(mesh):
    return jax.shard_map(
        on_device,
        mesh=mesh,
        in_specs=(
            P(None, "wide", "mid", "low", None),
            P(),
            P(),
            P(),
            P("wide", "mid", "low", None),
            P(),
            P(),
        ),
        out_specs=P(None, "wide", "mid", "low", None),
        check_vma=False,
    )
```

```python
from functools import partial

import jax
import jax.numpy as jnp
from jax import lax
from jax.experimental import pallas as pl
from jax.experimental.pallas import tpu as pltpu
from jax.sharding import PartitionSpec as P

HIGH = lax.Precision.HIGHEST
BUSY = 1 << 29
LONG = 1 << 32
AXES = ("wide", "mid", "low")
VSPEC = pl.BlockSpec(memory_space=pltpu.VMEM)
SSPEC = pl.BlockSpec(memory_space=pltpu.SMEM)


def split(value):
    high = value.astype(jnp.bfloat16)
    return high, (value - high.astype(jnp.float32)).astype(jnp.bfloat16)


def embed(value):
    half = value.shape[1] // 2
    return jnp.concatenate([value, jnp.concatenate([-value[:, half:], value[:, :half]], 1)], 0)


def dot(left, right, transposed=False):
    dims = (((1,), (1 if transposed else 0,)), ((), ()))
    return lax.dot_general(left, right, dims, preferred_element_type=jnp.float32)


def product(left, right, transposed=False):
    rows = left[0].shape[0]
    both = dot(jnp.concatenate(left, 0), right[0], transposed)
    return both[:rows] + both[rows:] + dot(left[0], right[1], transposed)


def complex_product(left, right):
    return product(left, tuple(embed(part) for part in right))


COSINE = (
    1.0,
    -0.5,
    0.0416666641831398,
    -0.0013888862449675798,
    2.480054899933748e-05,
    -2.753473324901279e-07,
    2.0603068140445657e-09,
    -9.720916779865085e-12,
)
SINE = (
    1.0,
    -0.1666666716337204,
    0.00833333283662796,
    -0.00019841254106722772,
    2.7556700388231548e-06,
    -2.5038662698761982e-08,
    1.5896317595576193e-10,
    -6.609633630347278e-13,
)


def series(square, terms):
    power = square
    terms = list(terms)
    while len(terms) > 1:
        terms = [terms[k] + terms[k + 1] * power for k in range(0, len(terms), 2)]
        power = power * power
    return terms[0]


def cosine_sine(angle):
    square = angle * angle
    return series(square, COSINE), angle * series(square, SINE)


def turn(value, angle):
    half = value.shape[1] // 2
    cosine, sine = cosine_sine(angle)
    real, imag = value[:, :half], value[:, half:]
    return jnp.concatenate([real * cosine - imag * sine, real * sine + imag * cosine], 1)


def side(ref, first=0):
    return jnp.concatenate([ref[first], ref[first + 1]], 1)


def gate(gates, number):
    return side(gates, 2 * number)


def scalars(ref):
    value = ref[...]
    return [value[0, place] for place in range(value.shape[1])]


class Plan:
    def __init__(self, rows, wide_count):
        self.rows = rows
        self.row_bits = rows.bit_length() - 1
        self.wide_bits = wide_count.bit_length() - 1
        self.low_base = self.row_bits - self.wide_bits - 3
        self.chunk = rows // (2 * wide_count)
        half = wide_count // 2
        tops = [tuple(range(k, min(k + 2, wide_count))) for k in range(half, wide_count, 2)]
        self.steps = [((pair[0], pair[-1]), (0, 1)) for pair in tops]
        self.steps += [((pair[1], pair[0]), (0, 1)) for pair in tops if len(pair) == 2]
        near = range(half - 1, 0, -1)
        self.steps += [((offset, offset), (1, 1)) for offset in near]
        self.steps.append(((0, 0), (1, 1)))
        self.steps += [((offset, offset), (0, 0)) for offset in near]
        self.shared = [step for step in self.steps if step[1][0] != step[1][1]]
        self.direct = [step for step in self.steps if step[1][0] == step[1][1]]


def choose(flag, pair):
    return pair[0] if pair[0] == pair[1] else pair[0] ^ (flag * (pair[0] ^ pair[1]))


def free_row(plan, inner, swap):
    base = plan.low_base
    lower = base + jnp.where(swap == 0, 1, 0)
    upper = base + jnp.where(swap == 2, 1, 2)
    return (
        (inner & ((1 << base) - 1))
        | jnp.left_shift(jnp.right_shift(inner, base) & 1, lower)
        | jnp.left_shift(jnp.right_shift(inner, base + 1) & 1, upper)
    )


def bits(value, place, count=1):
    return jnp.right_shift(value, place) & ((1 << count) - 1)


def sent_rows(plan, swaps, order):
    wide, core, low = lax.axis_index("wide"), lax.axis_index("mid") & 1, lax.axis_index("low") & 1
    targets = [(wide, low, core)]
    half = wide >> (plan.wide_bits - 1)
    for step in plan.steps:
        to_wide, to_low = wide ^ choose(half, step[0]), low ^ choose(core, step[1])
        for to_core in (core, 1 - core)[: 2 if step in plan.shared else 1]:
            targets.append((to_wide, to_low, to_core))
    base = plan.row_bits - 4
    position = plan.row_bits - 3 + swaps[0]
    places = [base + order[place] for place in range(4)]

    def reorder(row):
        old = row & ((1 << base) - 1)
        for place in range(4):
            old |= jnp.left_shift(bits(row, base + place), places[place])
        return old & ~jnp.left_shift(1, position), bits(old, position)

    inner = lax.broadcasted_iota(jnp.int32, (plan.chunk, plan.rows), 0)
    inner, inner_core = reorder(free_row(plan, inner, swaps[1]))
    result = []
    for to_wide, to_low, to_core in targets:
        outer = jnp.left_shift(to_low, plan.low_base + swaps[1])
        outer, outer_core = reorder(outer | (to_wide << (plan.row_bits - plan.wide_bits)))
        outer |= jnp.left_shift(to_core, position)
        result.append((inner | outer, inner_core | outer_core))
    return result


def received_rows(plan, swaps):
    wide, core, low = lax.axis_index("wide"), lax.axis_index("mid") & 1, lax.axis_index("low") & 1
    half = wide >> (plan.wide_bits - 1)
    sources = [(wide, low)]
    for server, steps in ((core, plan.shared), (core, plan.direct), (1 - core, plan.shared)):
        for step in steps:
            sources.append((wide ^ choose(1 - half, step[0]), low ^ choose(server, step[1])))
    inner = lax.broadcasted_iota(jnp.int32, (plan.chunk, plan.rows), 0)
    inner = free_row(plan, inner, swaps[1])
    result = []
    for from_wide, from_low in sources:
        outer = jnp.left_shift(from_low, plan.low_base + swaps[1])
        result.append(inner | outer | (from_wide << (plan.row_bits - plan.wide_bits)))
    return result


def one_hot(plan, chunks):
    column = lax.broadcasted_iota(jnp.int32, (plan.chunk, plan.rows), 1)
    return jnp.concatenate([(column == rows).astype(jnp.bfloat16) for rows in chunks], 0)


def phase_kernel(plan, phase_top, factors):
    cosine, sine = cosine_sine(jnp.full(factors.shape, phase_top[0, 0, 0, 0]))
    first = lax.broadcasted_iota(jnp.int32, factors.shape, 0) == 0
    factors[...] = jnp.where(first, cosine, sine)


def spin(value, factors):
    half = value.shape[1] // 2
    cosine, sine = factors[:1], factors[1:2]
    real, imag = value[:, :half], value[:, half:]
    return jnp.concatenate([real * cosine - imag * sine, real * sine + imag * cosine], 1)


def front_kernel(plan, state, factors, gates, angle, swaps, order, own, high, low):
    chunks = sent_rows(plan, scalars(swaps), scalars(order))
    chosen = one_hot(plan, [rows for rows, _ in chunks])
    core = lax.axis_index("mid") & 1
    mask = jnp.concatenate([(held == core).astype(jnp.float32) for _, held in chunks], 0)
    mask = jnp.concatenate([mask, mask], 1)
    outer = tuple(dot(chosen, part).astype(jnp.bfloat16) for part in split(gate(gates, 3)))
    inner = turn(gate(gates, 1), angle[...])
    merged = complex_product(outer, split(inner))
    own[...] = spin(complex_product(split(merged * mask), split(side(state))), factors[...])
    high[...], low[...] = split(merged * (1.0 - mask))


def send_kernel(plan, own, high, low, state, factors, *sent):
    total = complex_product((high[...], low[...]), split(side(state)))
    total = own[...] + spin(total, factors[...])
    start = 0
    for ref in sent:
        ref[...] = total[start : start + ref.shape[0]]
        start += ref.shape[0]


def chain(factors):
    while len(factors) > 1:
        pairs = [factors[k : k + 2] for k in range(0, len(factors), 2)]
        factors = [
            complex_product(split(pair[0]), split(pair[1])) if len(pair) == 2 else pair[0]
            for pair in pairs
        ]
    return factors[0]


def right_kernel(plan, count, gates, phase_low, high, low):
    factors = [gate(gates, number) for number in range((count - 1) // 2 * 2, 2, -2)]
    value = chain(factors + [turn(gate(gates, 2), phase_low[...]), gate(gates, 0)])
    real, imag = value[:, : plan.rows], value[:, plan.rows :]
    high[...], low[...] = split(
        jnp.concatenate(
            [jnp.concatenate([real, -imag], 1), jnp.concatenate([imag, real], 1)], 0
        )
    )


def left_kernel(plan, count, gates, swaps, high, low):
    placed = one_hot(plan, received_rows(plan, scalars(swaps)))
    first = gate(gates, 5)
    first = [
        sum(dot(part, placed, True) for part in split(half))
        for half in (first[:, : plan.rows], first[:, plan.rows :])
    ]
    factors = [gate(gates, number) for number in range((count - 2) // 2 * 2 + 1, 5, -2)]
    high[...], low[...] = split(chain(factors + [jnp.concatenate(first, 1)]))


def back_kernel(plan, count, gates, phase_low, swaps, kept, *factors):
    del kept
    right_kernel(plan, count, gates, phase_low, *factors[:2])
    left_kernel(plan, count, gates, swaps, *factors[2:])


def right_only(plan, count, gates, phase_low, kept, *out):
    right_kernel(plan, count, gates, phase_low, *out)


def left_only(plan, count, gates, swaps, kept, *out):
    left_kernel(plan, count, gates, swaps, *out)


def sort_kernel(plan, *refs):
    give = refs[-1]
    for place, ref in enumerate(refs[: len(plan.shared)]):
        give[place * plan.chunk : (place + 1) * plan.chunk] = ref[plan.chunk :]


def kept_kernel(plan, count, gates, swaps, give, *refs):
    del give
    *parts, right_high, right_low, left_high, left_low, high, low = refs
    left_kernel(plan, count, gates, swaps, left_high, left_low)
    value = jnp.concatenate([ref[: plan.chunk] for ref in parts], 0)
    value = product(split(value), (right_high[...], right_low[...]), True)
    high[...], low[...] = split(value)


def last_kernel(plan, high, low, *refs):
    *parts, right_high, right_low, left_high, left_low, out = refs
    value = jnp.concatenate([ref[...] for ref in parts], 0)
    value = split(product(split(value), (right_high[...], right_low[...]), True))
    value = tuple(jnp.concatenate([a[...], b], 0) for a, b in zip((high, low), value))
    result = complex_product((left_high[...], left_low[...]), value)
    half = plan.rows
    out[0] = result[:, :half]
    out[1] = result[:, half:]


def call(kernel, shapes, args, specs, flops=0):
    args = [
        arg if spec is SSPEC else pltpu.with_memory_space_constraint(arg, spec.memory_space)
        for arg, spec in zip(args, specs)
    ]
    return pl.pallas_call(
        kernel,
        out_shape=[pltpu.VMEM(shape, dtype) for shape, dtype in shapes],
        in_specs=specs,
        out_specs=[VSPEC] * len(shapes),
        cost_estimate=pl.CostEstimate(flops=flops, bytes_accessed=1 << 17, transcendentals=0),
    )(*args)


def exchange(value, step=((0, 0), (0, 0)), flip=0):
    wides, mids, lows = (lax.axis_size(axis) for axis in AXES)
    pairs = []
    for wide in range(wides):
        for mid in range(mids):
            for low in range(lows):
                to_wide = wide ^ step[0][2 * wide // wides]
                to = (to_wide * mids + (mid ^ flip)) * lows + (low ^ step[1][mid & 1])
                pairs.append(((wide * mids + mid) * lows + low, to))
    return lax.ppermute(value, AXES, pairs)


def merged_device(state, gates, phase_low, phase_mid, phase_top, swap_qubits, regroup_order):
    rows = gates.shape[-1]
    plan = Plan(rows, lax.axis_size("wide"))
    chunk = plan.chunk
    f32, bf16 = jnp.float32, jnp.bfloat16
    gates = gates.reshape(-1, rows, rows)
    swaps, order = swap_qubits.reshape(1, -1), regroup_order.reshape(1, -1)
    square = state.reshape(2, rows, rows)
    other = exchange(square, flip=1)
    (factors,) = call(partial(phase_kernel, plan), [((8, rows), f32)], (phase_top,), (SSPEC,), BUSY)
    other_factors = exchange(factors, flip=1)
    own, high, low = call(
        partial(front_kernel, plan),
        [((rows, 2 * rows), f32), ((rows, 2 * rows), bf16), ((rows, 2 * rows), bf16)],
        (square, factors, gates, phase_mid.reshape(1, rows), swaps, order),
        (VSPEC,) * 6,
    )
    shapes = [(chunk, 2 * rows)]
    shapes += [(2 * chunk if step in plan.shared else chunk, 2 * rows) for step in plan.steps]
    local, *sent = call(
        partial(send_kernel, plan),
        [(shape, f32) for shape in shapes],
        (own, high, low, other, other_factors),
        (VSPEC,) * 5,
    )
    received = [exchange(value, step) for value, step in zip(sent, plan.steps)]
    right_high, right_low = call(
        partial(right_only, plan, gates.shape[0] // 2),
        [((2 * rows, 2 * rows), bf16)] * 2,
        (gates, phase_low.reshape(1, rows), local),
        (VSPEC,) * 3,
    )
    shared = [value for value, step in zip(received, plan.steps) if step in plan.shared]
    (give,) = call(
        partial(sort_kernel, plan),
        [((len(plan.shared) * chunk, 2 * rows), f32)],
        (*shared, right_low),
        (VSPEC,) * (len(shared) + 1),
    )
    given = exchange(give, flip=1)
    kept_rows = (1 + len(shared)) * chunk
    left_high, left_low, high, low = call(
        partial(kept_kernel, plan, gates.shape[0] // 2),
        [((rows, 2 * rows), bf16)] * 2 + [((kept_rows, 2 * rows), bf16)] * 2,
        (gates, swaps, give, local, *shared, right_high, right_low),
        (VSPEC,) * (len(shared) + 6),
        LONG,
    )
    direct = [value for value, step in zip(received, plan.steps) if step in plan.direct]
    args = (high, low, *direct, given, right_high, right_low, left_high, left_low)
    out = pl.pallas_call(
        partial(last_kernel, plan),
        out_shape=jax.ShapeDtypeStruct((2, rows, rows), f32),
        in_specs=[VSPEC] * len(args),
    )(*[pltpu.with_memory_space_constraint(arg, pltpu.VMEM) for arg in args])
    return out.reshape(state.shape)


def partner(value, axis, stride):
    mask = 2**stride
    pairs = [(source, source ^ mask) for source in range(lax.axis_size(axis))]
    return lax.ppermute(value, axis, pairs)


def gate_inner(vector, real_gate, imag_gate):

    def product(values, matrix):
        return jnp.einsum("...b,ab->...a", values, matrix, precision=HIGH)

    real_part, imag_part = (vector[0], vector[1])
    return jnp.stack(
        [
            product(real_part, real_gate) - product(imag_part, imag_gate),
            product(real_part, imag_gate) + product(imag_part, real_gate),
        ]
    )


def gate_outer(vector, real_gate, imag_gate):

    def product(values, matrix):
        return jnp.einsum("ab,rbc->rac", matrix, values, precision=HIGH)

    real_part, imag_part = (vector[0], vector[1])
    return jnp.stack(
        [
            product(real_part, real_gate) - product(imag_part, imag_gate),
            product(real_part, imag_gate) + product(imag_part, real_gate),
        ]
    )


def apply_gate(vector, gates, number, gate_len):
    if number % 2 == 0:
        result = gate_inner(vector.reshape(2, -1, gate_len), gates[number, 0], gates[number, 1])
    else:
        result = gate_outer(
            vector.reshape(2, -1, gate_len, gate_len), gates[number, 0], gates[number, 1]
        )
    return result.reshape(2, -1)


def half_rows(vector, offset, base, own_bit, local_len):
    counter = jnp.arange(4, dtype=jnp.int32)
    lower = counter & jnp.left_shift(1, offset) - 1
    higher = jnp.right_shift(counter, offset)
    row_index = jnp.left_shift(higher, offset + 1) | jnp.left_shift(1 - own_bit, offset) | lower
    blocks = vector.reshape(2, local_len >> base + 3, 8, 1 << base)
    return (blocks, row_index, jnp.take(blocks, row_index, axis=2))


def move_bits(vector, lower, upper, local_len):
    if lower == upper:
        return vector
    shaped = vector.reshape(2, local_len >> upper + 1, 2, 1 << upper - lower - 1, 2, 1 << lower)
    return jnp.swapaxes(shaped, 2, 4).reshape(2, local_len)


def general_device(state, gates, phase_low, phase_mid, phase_top, swap_qubits, regroup_order):
    local_len = state.shape[-1]
    gate_len = gates.shape[-1]
    gate_count = gates.shape[0]
    local_bits = local_len.bit_length() - 1
    upper_len = local_len // (gate_len * gate_len)
    wide_count = lax.axis_size("wide")
    wide_bits = wide_count.bit_length() - 1
    vector = apply_gate(state.reshape(2, -1), gates, 0, gate_len)
    vector = vector.reshape(2, upper_len, gate_len, gate_len)
    angle = (
        phase_top.reshape(upper_len)[:, None, None]
        + phase_mid[None, :, None]
        + phase_low[None, None, :]
    )
    cosine = jnp.cos(angle)
    sine_part = jnp.sin(angle)
    vector = jnp.stack(
        [vector[0] * cosine - vector[1] * sine_part, vector[0] * sine_part + vector[1] * cosine]
    ).reshape(2, -1)
    for number in range(1, 4):
        vector = apply_gate(vector, gates, number, gate_len)
    mid_bit = lax.axis_index("mid") & 1
    blocks, row_index, sent_half = half_rows(
        vector, swap_qubits[0], local_bits - 3, mid_bit, local_len
    )
    received = partner(sent_half, "mid", 0)
    vector = blocks.at[:, :, row_index].set(received).reshape(2, local_len)
    row_ids = jnp.arange(16, dtype=jnp.int32)[:, None]
    row_bits = jnp.right_shift(row_ids, jnp.arange(4, dtype=jnp.int32)[None, :]) & 1
    order_index = jnp.sum(jnp.left_shift(row_bits, regroup_order[None, :]), axis=1)
    vector = jnp.take(vector.reshape(2, 16, local_len // 16), order_index, axis=1).reshape(
        2, local_len
    )
    low_base = local_bits - wide_bits - 3
    target = low_base + 2
    branches = [
        partial(move_bits, lower=low_base + place, upper=target, local_len=local_len)
        for place in range(3)
    ]
    vector = lax.switch(swap_qubits[1], branches, vector)
    shaped = vector.reshape(2, wide_count, 2, local_len // (2 * wide_count))
    moved = lax.all_to_all(
        lax.all_to_all(shaped, "wide", split_axis=1, concat_axis=1, tiled=True),
        "low",
        split_axis=2,
        concat_axis=2,
        tiled=True,
    )
    vector = lax.switch(swap_qubits[1], branches, moved.reshape(2, local_len))
    for number in range(4, gate_count):
        vector = apply_gate(vector, gates, number, gate_len)
    return vector.reshape(state.shape)


def on_device(state, gates, *rest):
    rows = gates.shape[-1]
    sizes = [lax.axis_size(axis) for axis in AXES]
    base = rows.bit_length() - sizes[0].bit_length() - 3
    merged = state.shape[-1] == rows * rows and base >= 2 and min(sizes) >= 2
    return (merged_device if merged else general_device)(state, gates, *rest)


def solution(mesh):
    return jax.shard_map(
        on_device,
        mesh=mesh,
        in_specs=(
            P(None, "wide", "mid", "low", None),
            P(),
            P(),
            P(),
            P("wide", "mid", "low", None),
            P(),
            P(),
        ),
        out_specs=P(None, "wide", "mid", "low", None),
        check_vma=False,
    )
```

```python
from functools import partial

import jax
import jax.numpy as jnp
from jax import lax
from jax.experimental import pallas as pl
from jax.experimental.pallas import tpu as pltpu
from jax.sharding import PartitionSpec as P

HIGH = lax.Precision.HIGHEST
BUSY = 1 << 29
LONG = 1 << 32
AXES = ("wide", "mid", "low")
VSPEC = pl.BlockSpec(memory_space=pltpu.VMEM)
SSPEC = pl.BlockSpec(memory_space=pltpu.SMEM)


def split(value):
    high = value.astype(jnp.bfloat16)
    return high, (value - high.astype(jnp.float32)).astype(jnp.bfloat16)


def embed(value):
    half = value.shape[1] // 2
    return jnp.concatenate([value, jnp.concatenate([-value[:, half:], value[:, :half]], 1)], 0)


def dot(left, right, transposed=False):
    dims = (((1,), (1 if transposed else 0,)), ((), ()))
    return lax.dot_general(left, right, dims, preferred_element_type=jnp.float32)


def product(left, right, transposed=False):
    rows = left[0].shape[0]
    both = dot(jnp.concatenate(left, 0), right[0], transposed)
    return both[:rows] + both[rows:] + dot(left[0], right[1], transposed)


def complex_product(left, right):
    return product(left, tuple(embed(part) for part in right))


COSINE = (
    1.0,
    -0.5,
    0.0416666641831398,
    -0.0013888862449675798,
    2.480054899933748e-05,
    -2.753473324901279e-07,
    2.0603068140445657e-09,
    -9.720916779865085e-12,
)
SINE = (
    1.0,
    -0.1666666716337204,
    0.00833333283662796,
    -0.00019841254106722772,
    2.7556700388231548e-06,
    -2.5038662698761982e-08,
    1.5896317595576193e-10,
    -6.609633630347278e-13,
)


def series(square, terms):
    power = square
    terms = list(terms)
    while len(terms) > 1:
        terms = [terms[k] + terms[k + 1] * power for k in range(0, len(terms), 2)]
        power = power * power
    return terms[0]


def cosine_sine(angle):
    square = angle * angle
    return series(square, COSINE), angle * series(square, SINE)


def turn(value, angle):
    half = value.shape[1] // 2
    cosine, sine = cosine_sine(angle)
    real, imag = value[:, :half], value[:, half:]
    return jnp.concatenate([real * cosine - imag * sine, real * sine + imag * cosine], 1)


def side(ref, first=0):
    return jnp.concatenate([ref[first], ref[first + 1]], 1)


def gate(gates, number):
    return side(gates, 2 * number)


def scalars(ref):
    value = ref[...]
    return [value[0, place] for place in range(value.shape[1])]


class Plan:
    def __init__(self, rows, wide_count):
        self.rows = rows
        self.row_bits = rows.bit_length() - 1
        self.wide_bits = wide_count.bit_length() - 1
        self.low_base = self.row_bits - self.wide_bits - 3
        self.chunk = rows // (2 * wide_count)
        half = wide_count // 2
        tops = [tuple(range(k, min(k + 2, wide_count))) for k in range(half, wide_count, 2)]
        half = wide_count // 2
        tops = [tuple(range(k, min(k + 2, wide_count))) for k in range(half, wide_count, 2)]
        pairs = [(pair[0], pair[-1]) for pair in tops]
        pairs += [(pair[1], pair[0]) for pair in tops if len(pair) == 2]
        pairs += [(offset, offset) for offset in range(half - 1, 1, -1)]
        self.steps = [((*pair, 0), (*pair, 1)) for pair in pairs]
        if half > 1:
            self.steps += [((1, 1, 0), (0, 0, 1)), ((1, 1, 1), (1, 1, 1))]
        else:
            self.steps.append(((0, 0, 1), (0, 0, 1)))
        self.shared = [step for step in self.steps if step[0] != step[1]]
        self.direct = [step for step in self.steps if step[0] == step[1]]


def partner(step, core, half, wide, low):
    entries = [(low_part, a ^ (half * (a ^ b))) for a, b, low_part in step]
    low_part, wide_part = [a ^ (core * (a ^ b)) for a, b in zip(*entries)]
    return wide ^ wide_part, low ^ low_part


def free_row(plan, inner, swap):
    base = plan.low_base
    lower = base + jnp.where(swap == 0, 1, 0)
    upper = base + jnp.where(swap == 2, 1, 2)
    return (
        (inner & ((1 << base) - 1))
        | jnp.left_shift(jnp.right_shift(inner, base) & 1, lower)
        | jnp.left_shift(jnp.right_shift(inner, base + 1) & 1, upper)
    )


def bits(value, place, count=1):
    return jnp.right_shift(value, place) & ((1 << count) - 1)


def sent_rows(plan, swaps, order):
    wide, core, low = lax.axis_index("wide"), lax.axis_index("mid") & 1, lax.axis_index("low") & 1
    targets = [(wide, low, core)]
    half = wide >> (plan.wide_bits - 1)
    for step in plan.steps:
        chip = partner(step, core, half, wide, low)
        for to_core in (core, 1 - core)[: 2 if step in plan.shared else 1]:
            targets.append((*chip, to_core))
    base = plan.row_bits - 4
    position = plan.row_bits - 3 + swaps[0]
    places = [base + order[place] for place in range(4)]

    def reorder(row):
        old = row & ((1 << base) - 1)
        for place in range(4):
            old |= jnp.left_shift(bits(row, base + place), places[place])
        return old & ~jnp.left_shift(1, position), bits(old, position)

    inner = lax.broadcasted_iota(jnp.int32, (plan.chunk, plan.rows), 0)
    inner, inner_core = reorder(free_row(plan, inner, swaps[1]))
    result = []
    for to_wide, to_low, to_core in targets:
        outer = jnp.left_shift(to_low, plan.low_base + swaps[1])
        outer, outer_core = reorder(outer | (to_wide << (plan.row_bits - plan.wide_bits)))
        outer |= jnp.left_shift(to_core, position)
        result.append((inner | outer, inner_core | outer_core))
    return result


def received_rows(plan, swaps):
    wide, core, low = lax.axis_index("wide"), lax.axis_index("mid") & 1, lax.axis_index("low") & 1
    half = wide >> (plan.wide_bits - 1)
    sources = [(wide, low)]
    for server, steps in ((core, plan.shared), (core, plan.direct), (1 - core, plan.shared)):
        for step in steps:
            sources.append(partner(step, server, 1 - half, wide, low))
    inner = lax.broadcasted_iota(jnp.int32, (plan.chunk, plan.rows), 0)
    inner = free_row(plan, inner, swaps[1])
    result = []
    for from_wide, from_low in sources:
        outer = jnp.left_shift(from_low, plan.low_base + swaps[1])
        result.append(inner | outer | (from_wide << (plan.row_bits - plan.wide_bits)))
    return result


def one_hot(plan, chunks):
    column = lax.broadcasted_iota(jnp.int32, (plan.chunk, plan.rows), 1)
    return jnp.concatenate([(column == rows).astype(jnp.bfloat16) for rows in chunks], 0)


def phase_kernel(plan, phase_top, factors):
    cosine, sine = cosine_sine(jnp.full(factors.shape, phase_top[0, 0, 0, 0]))
    first = lax.broadcasted_iota(jnp.int32, factors.shape, 0) == 0
    factors[...] = jnp.where(first, cosine, sine)


def spin(value, factors):
    half = value.shape[1] // 2
    cosine, sine = factors[:1], factors[1:2]
    real, imag = value[:, :half], value[:, half:]
    return jnp.concatenate([real * cosine - imag * sine, real * sine + imag * cosine], 1)


def front_kernel(plan, state, factors, gates, angle, swaps, order, own, high, low):
    chunks = sent_rows(plan, scalars(swaps), scalars(order))
    chosen = one_hot(plan, [rows for rows, _ in chunks])
    core = lax.axis_index("mid") & 1
    mask = jnp.concatenate([(held == core).astype(jnp.float32) for _, held in chunks], 0)
    mask = jnp.concatenate([mask, mask], 1)
    outer = tuple(dot(chosen, part).astype(jnp.bfloat16) for part in split(gate(gates, 3)))
    inner = turn(gate(gates, 1), angle[...])
    merged = complex_product(outer, split(inner))
    own[...] = spin(complex_product(split(merged * mask), split(side(state))), factors[...])
    high[...], low[...] = split(merged * (1.0 - mask))


def send_kernel(plan, own, high, low, state, factors, *sent):
    total = complex_product((high[...], low[...]), split(side(state)))
    total = own[...] + spin(total, factors[...])
    start = 0
    for ref in sent:
        ref[...] = total[start : start + ref.shape[0]]
        start += ref.shape[0]


def chain(factors):
    while len(factors) > 1:
        pairs = [factors[k : k + 2] for k in range(0, len(factors), 2)]
        factors = [
            complex_product(split(pair[0]), split(pair[1])) if len(pair) == 2 else pair[0]
            for pair in pairs
        ]
    return factors[0]


def right_kernel(plan, count, gates, phase_low, high, low):
    factors = [gate(gates, number) for number in range((count - 1) // 2 * 2, 2, -2)]
    value = chain(factors + [turn(gate(gates, 2), phase_low[...]), gate(gates, 0)])
    real, imag = value[:, : plan.rows], value[:, plan.rows :]
    high[...], low[...] = split(
        jnp.concatenate(
            [jnp.concatenate([real, -imag], 1), jnp.concatenate([imag, real], 1)], 0
        )
    )


def left_kernel(plan, count, gates, swaps, high, low):
    placed = one_hot(plan, received_rows(plan, scalars(swaps)))
    first = gate(gates, 5)
    first = [
        sum(dot(part, placed, True) for part in split(half))
        for half in (first[:, : plan.rows], first[:, plan.rows :])
    ]
    factors = [gate(gates, number) for number in range((count - 2) // 2 * 2 + 1, 5, -2)]
    high[...], low[...] = split(chain(factors + [jnp.concatenate(first, 1)]))


def back_kernel(plan, count, gates, phase_low, swaps, kept, *factors):
    del kept
    right_kernel(plan, count, gates, phase_low, *factors[:2])
    left_kernel(plan, count, gates, swaps, *factors[2:])


def right_only(plan, count, gates, phase_low, kept, *out):
    right_kernel(plan, count, gates, phase_low, *out)


def left_only(plan, count, gates, swaps, kept, *out):
    left_kernel(plan, count, gates, swaps, *out)


def sort_kernel(plan, *refs):
    give = refs[-1]
    for place, ref in enumerate(refs[: len(plan.shared)]):
        give[place * plan.chunk : (place + 1) * plan.chunk] = ref[plan.chunk :]


def kept_kernel(plan, count, gates, swaps, give, *refs):
    del give
    *parts, right_high, right_low, left_high, left_low, high, low = refs
    left_kernel(plan, count, gates, swaps, left_high, left_low)
    value = jnp.concatenate([ref[: plan.chunk] for ref in parts], 0)
    value = product(split(value), (right_high[...], right_low[...]), True)
    high[...], low[...] = split(value)


def last_kernel(plan, high, low, *refs):
    *parts, right_high, right_low, left_high, left_low, out = refs
    value = jnp.concatenate([ref[...] for ref in parts], 0)
    value = split(product(split(value), (right_high[...], right_low[...]), True))
    value = tuple(jnp.concatenate([a[...], b], 0) for a, b in zip((high, low), value))
    result = complex_product((left_high[...], left_low[...]), value)
    half = plan.rows
    out[0] = result[:, :half]
    out[1] = result[:, half:]


def call(kernel, shapes, args, specs, flops=0):
    args = [
        arg if spec is SSPEC else pltpu.with_memory_space_constraint(arg, spec.memory_space)
        for arg, spec in zip(args, specs)
    ]
    return pl.pallas_call(
        kernel,
        out_shape=[pltpu.VMEM(shape, dtype) for shape, dtype in shapes],
        in_specs=specs,
        out_specs=[VSPEC] * len(shapes),
        cost_estimate=pl.CostEstimate(flops=flops, bytes_accessed=1 << 17, transcendentals=0),
    )(*args)


def exchange(value, step=((0, 0, 0), (0, 0, 0)), flip=0):
    wides, mids, lows = (lax.axis_size(axis) for axis in AXES)
    pairs = []
    for wide in range(wides):
        for mid in range(mids):
            for low in range(lows):
                *offsets, low_part = step[mid & 1]
                to_wide = wide ^ offsets[2 * wide // wides]
                to = (to_wide * mids + (mid ^ flip)) * lows + (low ^ low_part)
                pairs.append(((wide * mids + mid) * lows + low, to))
    return lax.ppermute(value, AXES, pairs)


def merged_device(state, gates, phase_low, phase_mid, phase_top, swap_qubits, regroup_order):
    rows = gates.shape[-1]
    plan = Plan(rows, lax.axis_size("wide"))
    chunk = plan.chunk
    f32, bf16 = jnp.float32, jnp.bfloat16
    gates = gates.reshape(-1, rows, rows)
    swaps, order = swap_qubits.reshape(1, -1), regroup_order.reshape(1, -1)
    square = state.reshape(2, rows, rows)
    other = exchange(square, flip=1)
    (factors,) = call(partial(phase_kernel, plan), [((8, rows), f32)], (phase_top,), (SSPEC,), BUSY)
    other_factors = exchange(factors, flip=1)
    own, high, low = call(
        partial(front_kernel, plan),
        [((rows, 2 * rows), f32), ((rows, 2 * rows), bf16), ((rows, 2 * rows), bf16)],
        (square, factors, gates, phase_mid.reshape(1, rows), swaps, order),
        (VSPEC,) * 6,
    )
    shapes = [(chunk, 2 * rows)]
    shapes += [(2 * chunk if step in plan.shared else chunk, 2 * rows) for step in plan.steps]
    local, *sent = call(
        partial(send_kernel, plan),
        [(shape, f32) for shape in shapes],
        (own, high, low, other, other_factors),
        (VSPEC,) * 5,
    )
    received = [exchange(value, step) for value, step in zip(sent, plan.steps)]
    right_high, right_low = call(
        partial(right_only, plan, gates.shape[0] // 2),
        [((2 * rows, 2 * rows), bf16)] * 2,
        (gates, phase_low.reshape(1, rows), local),
        (VSPEC,) * 3,
    )
    shared = [value for value, step in zip(received, plan.steps) if step in plan.shared]
    (give,) = call(
        partial(sort_kernel, plan),
        [((len(plan.shared) * chunk, 2 * rows), f32)],
        (*shared, right_low),
        (VSPEC,) * (len(shared) + 1),
    )
    given = exchange(give, flip=1)
    kept_rows = (1 + len(shared)) * chunk
    left_high, left_low, high, low = call(
        partial(kept_kernel, plan, gates.shape[0] // 2),
        [((rows, 2 * rows), bf16)] * 2 + [((kept_rows, 2 * rows), bf16)] * 2,
        (gates, swaps, give, local, *shared, right_high, right_low),
        (VSPEC,) * (len(shared) + 6),
        LONG,
    )
    direct = [value for value, step in zip(received, plan.steps) if step in plan.direct]
    args = (high, low, *direct, given, right_high, right_low, left_high, left_low)
    out = pl.pallas_call(
        partial(last_kernel, plan),
        out_shape=jax.ShapeDtypeStruct((2, rows, rows), f32),
        in_specs=[VSPEC] * len(args),
    )(*[pltpu.with_memory_space_constraint(arg, pltpu.VMEM) for arg in args])
    return out.reshape(state.shape)


def mate(value, axis, stride):
    mask = 2**stride
    pairs = [(source, source ^ mask) for source in range(lax.axis_size(axis))]
    return lax.ppermute(value, axis, pairs)


def gate_inner(vector, real_gate, imag_gate):

    def product(values, matrix):
        return jnp.einsum("...b,ab->...a", values, matrix, precision=HIGH)

    real_part, imag_part = (vector[0], vector[1])
    return jnp.stack(
        [
            product(real_part, real_gate) - product(imag_part, imag_gate),
            product(real_part, imag_gate) + product(imag_part, real_gate),
        ]
    )


def gate_outer(vector, real_gate, imag_gate):

    def product(values, matrix):
        return jnp.einsum("ab,rbc->rac", matrix, values, precision=HIGH)

    real_part, imag_part = (vector[0], vector[1])
    return jnp.stack(
        [
            product(real_part, real_gate) - product(imag_part, imag_gate),
            product(real_part, imag_gate) + product(imag_part, real_gate),
        ]
    )


def apply_gate(vector, gates, number, gate_len):
    if number % 2 == 0:
        result = gate_inner(vector.reshape(2, -1, gate_len), gates[number, 0], gates[number, 1])
    else:
        result = gate_outer(
            vector.reshape(2, -1, gate_len, gate_len), gates[number, 0], gates[number, 1]
        )
    return result.reshape(2, -1)


def half_rows(vector, offset, base, own_bit, local_len):
    counter = jnp.arange(4, dtype=jnp.int32)
    lower = counter & jnp.left_shift(1, offset) - 1
    higher = jnp.right_shift(counter, offset)
    row_index = jnp.left_shift(higher, offset + 1) | jnp.left_shift(1 - own_bit, offset) | lower
    blocks = vector.reshape(2, local_len >> base + 3, 8, 1 << base)
    return (blocks, row_index, jnp.take(blocks, row_index, axis=2))


def move_bits(vector, lower, upper, local_len):
    if lower == upper:
        return vector
    shaped = vector.reshape(2, local_len >> upper + 1, 2, 1 << upper - lower - 1, 2, 1 << lower)
    return jnp.swapaxes(shaped, 2, 4).reshape(2, local_len)


def general_device(state, gates, phase_low, phase_mid, phase_top, swap_qubits, regroup_order):
    local_len = state.shape[-1]
    gate_len = gates.shape[-1]
    gate_count = gates.shape[0]
    local_bits = local_len.bit_length() - 1
    upper_len = local_len // (gate_len * gate_len)
    wide_count = lax.axis_size("wide")
    wide_bits = wide_count.bit_length() - 1
    vector = apply_gate(state.reshape(2, -1), gates, 0, gate_len)
    vector = vector.reshape(2, upper_len, gate_len, gate_len)
    angle = (
        phase_top.reshape(upper_len)[:, None, None]
        + phase_mid[None, :, None]
        + phase_low[None, None, :]
    )
    cosine = jnp.cos(angle)
    sine_part = jnp.sin(angle)
    vector = jnp.stack(
        [vector[0] * cosine - vector[1] * sine_part, vector[0] * sine_part + vector[1] * cosine]
    ).reshape(2, -1)
    for number in range(1, 4):
        vector = apply_gate(vector, gates, number, gate_len)
    mid_bit = lax.axis_index("mid") & 1
    blocks, row_index, sent_half = half_rows(
        vector, swap_qubits[0], local_bits - 3, mid_bit, local_len
    )
    received = mate(sent_half, "mid", 0)
    vector = blocks.at[:, :, row_index].set(received).reshape(2, local_len)
    row_ids = jnp.arange(16, dtype=jnp.int32)[:, None]
    row_bits = jnp.right_shift(row_ids, jnp.arange(4, dtype=jnp.int32)[None, :]) & 1
    order_index = jnp.sum(jnp.left_shift(row_bits, regroup_order[None, :]), axis=1)
    vector = jnp.take(vector.reshape(2, 16, local_len // 16), order_index, axis=1).reshape(
        2, local_len
    )
    low_base = local_bits - wide_bits - 3
    target = low_base + 2
    branches = [
        partial(move_bits, lower=low_base + place, upper=target, local_len=local_len)
        for place in range(3)
    ]
    vector = lax.switch(swap_qubits[1], branches, vector)
    shaped = vector.reshape(2, wide_count, 2, local_len // (2 * wide_count))
    moved = lax.all_to_all(
        lax.all_to_all(shaped, "wide", split_axis=1, concat_axis=1, tiled=True),
        "low",
        split_axis=2,
        concat_axis=2,
        tiled=True,
    )
    vector = lax.switch(swap_qubits[1], branches, moved.reshape(2, local_len))
    for number in range(4, gate_count):
        vector = apply_gate(vector, gates, number, gate_len)
    return vector.reshape(state.shape)


def on_device(state, gates, *rest):
    rows = gates.shape[-1]
    sizes = [lax.axis_size(axis) for axis in AXES]
    base = rows.bit_length() - sizes[0].bit_length() - 3
    merged = state.shape[-1] == rows * rows and base >= 2 and min(sizes) >= 2
    return (merged_device if merged else general_device)(state, gates, *rest)


def solution(mesh):
    return jax.shard_map(
        on_device,
        mesh=mesh,
        in_specs=(
            P(None, "wide", "mid", "low", None),
            P(),
            P(),
            P(),
            P("wide", "mid", "low", None),
            P(),
            P(),
        ),
        out_specs=P(None, "wide", "mid", "low", None),
        check_vma=False,
    )
```

```python
from functools import partial

import jax
import jax.numpy as jnp
from jax import lax
from jax.experimental import pallas as pl
from jax.experimental.pallas import tpu as pltpu
from jax.sharding import PartitionSpec as P

HIGH = lax.Precision.HIGHEST
BUSY = 1 << 29
LONG = 1 << 32
AXES = ("wide", "mid", "low")
VSPEC = pl.BlockSpec(memory_space=pltpu.VMEM)
SSPEC = pl.BlockSpec(memory_space=pltpu.SMEM)


def split(value):
    high = value.astype(jnp.bfloat16)
    return high, (value - high.astype(jnp.float32)).astype(jnp.bfloat16)


def embed(value):
    half = value.shape[1] // 2
    return jnp.concatenate([value, jnp.concatenate([-value[:, half:], value[:, :half]], 1)], 0)


def dot(left, right, transposed=False):
    dims = (((1,), (1 if transposed else 0,)), ((), ()))
    return lax.dot_general(left, right, dims, preferred_element_type=jnp.float32)


def product(left, right, transposed=False):
    rows = left[0].shape[0]
    both = dot(jnp.concatenate(left, 0), right[0], transposed)
    return both[:rows] + both[rows:] + dot(left[0], right[1], transposed)


def complex_product(left, right):
    return product(left, tuple(embed(part) for part in right))


COSINE = (
    1.0,
    -0.5,
    0.0416666641831398,
    -0.0013888862449675798,
    2.480054899933748e-05,
    -2.753473324901279e-07,
    2.0603068140445657e-09,
    -9.720916779865085e-12,
)
SINE = (
    1.0,
    -0.1666666716337204,
    0.00833333283662796,
    -0.00019841254106722772,
    2.7556700388231548e-06,
    -2.5038662698761982e-08,
    1.5896317595576193e-10,
    -6.609633630347278e-13,
)


def series(square, terms):
    power = square
    terms = list(terms)
    while len(terms) > 1:
        terms = [terms[k] + terms[k + 1] * power for k in range(0, len(terms), 2)]
        power = power * power
    return terms[0]


def cosine_sine(angle):
    square = angle * angle
    return series(square, COSINE), angle * series(square, SINE)


def turn(value, angle):
    half = value.shape[1] // 2
    cosine, sine = cosine_sine(angle)
    real, imag = value[:, :half], value[:, half:]
    return jnp.concatenate([real * cosine - imag * sine, real * sine + imag * cosine], 1)


def side(ref, first=0):
    return jnp.concatenate([ref[first], ref[first + 1]], 1)


def gate(gates, number):
    return side(gates, 2 * number)


def scalars(ref):
    value = ref[...]
    return [value[0, place] for place in range(value.shape[1])]


class Plan:
    def __init__(self, rows, wide_count):
        self.rows = rows
        self.row_bits = rows.bit_length() - 1
        self.wide_bits = wide_count.bit_length() - 1
        self.low_base = self.row_bits - self.wide_bits - 3
        self.chunk = rows // (2 * wide_count)
        half = wide_count // 2
        tops = [tuple(range(k, min(k + 2, wide_count))) for k in range(half, wide_count, 2)]
        half = wide_count // 2
        tops = [tuple(range(k, min(k + 2, wide_count))) for k in range(half, wide_count, 2)]
        pairs = [(pair[0], pair[-1]) for pair in tops]
        pairs += [(pair[1], pair[0]) for pair in tops if len(pair) == 2]
        pairs += [(offset, offset) for offset in range(half - 1, 1, -1)]
        self.steps = [((*pair, 0), (*pair, 1)) for pair in pairs]
        if half > 1:
            self.steps += [((1, 1, 0), (0, 0, 1)), ((1, 1, 1), (1, 1, 1))]
        else:
            self.steps.append(((0, 0, 1), (0, 0, 1)))
        self.shared = [step for step in self.steps if step[0] != step[1]]
        self.direct = [step for step in self.steps if step[0] == step[1]]


def partner(step, core, half, wide, low):
    entries = [(low_part, a ^ (half * (a ^ b))) for a, b, low_part in step]
    low_part, wide_part = [a ^ (core * (a ^ b)) for a, b in zip(*entries)]
    return wide ^ wide_part, low ^ low_part


def free_row(plan, inner, swap):
    base = plan.low_base
    lower = base + jnp.where(swap == 0, 1, 0)
    upper = base + jnp.where(swap == 2, 1, 2)
    return (
        (inner & ((1 << base) - 1))
        | jnp.left_shift(jnp.right_shift(inner, base) & 1, lower)
        | jnp.left_shift(jnp.right_shift(inner, base + 1) & 1, upper)
    )


def bits(value, place, count=1):
    return jnp.right_shift(value, place) & ((1 << count) - 1)


def sent_rows(plan, swaps, order):
    wide, core, low = lax.axis_index("wide"), lax.axis_index("mid") & 1, lax.axis_index("low") & 1
    targets = [(wide, low, core)]
    half = wide >> (plan.wide_bits - 1)
    for step in plan.steps:
        chip = partner(step, core, half, wide, low)
        for to_core in (core, 1 - core)[: 2 if step in plan.shared else 1]:
            targets.append((*chip, to_core))
    base = plan.row_bits - 4
    position = plan.row_bits - 3 + swaps[0]
    places = [base + order[place] for place in range(4)]

    def reorder(row):
        old = row & ((1 << base) - 1)
        for place in range(4):
            old |= jnp.left_shift(bits(row, base + place), places[place])
        return old & ~jnp.left_shift(1, position), bits(old, position)

    inner = lax.broadcasted_iota(jnp.int32, (plan.chunk, plan.rows), 0)
    inner, inner_core = reorder(free_row(plan, inner, swaps[1]))
    result = []
    for to_wide, to_low, to_core in targets:
        outer = jnp.left_shift(to_low, plan.low_base + swaps[1])
        outer, outer_core = reorder(outer | (to_wide << (plan.row_bits - plan.wide_bits)))
        outer |= jnp.left_shift(to_core, position)
        result.append((inner | outer, inner_core | outer_core))
    return result


def received_rows(plan, swaps):
    wide, core, low = lax.axis_index("wide"), lax.axis_index("mid") & 1, lax.axis_index("low") & 1
    half = wide >> (plan.wide_bits - 1)
    sources = [(wide, low)]
    for server, steps in ((core, plan.shared), (core, plan.direct), (1 - core, plan.shared)):
        for step in steps:
            sources.append(partner(step, server, 1 - half, wide, low))
    inner = lax.broadcasted_iota(jnp.int32, (plan.chunk, plan.rows), 0)
    inner = free_row(plan, inner, swaps[1])
    result = []
    for from_wide, from_low in sources:
        outer = jnp.left_shift(from_low, plan.low_base + swaps[1])
        result.append(inner | outer | (from_wide << (plan.row_bits - plan.wide_bits)))
    return result


def one_hot(plan, chunks):
    column = lax.broadcasted_iota(jnp.int32, (plan.chunk, plan.rows), 1)
    return jnp.concatenate([(column == rows).astype(jnp.bfloat16) for rows in chunks], 0)


def phase_kernel(plan, phase_top, factors):
    cosine, sine = cosine_sine(jnp.full(factors.shape, phase_top[0, 0, 0, 0]))
    first = lax.broadcasted_iota(jnp.int32, factors.shape, 0) == 0
    factors[...] = jnp.where(first, cosine, sine)


def spin(value, factors):
    half = value.shape[1] // 2
    cosine, sine = factors[:1], factors[1:2]
    real, imag = value[:, :half], value[:, half:]
    return jnp.concatenate([real * cosine - imag * sine, real * sine + imag * cosine], 1)


def load_kernel(state, factors, turned):
    turned[...] = spin(side(state), factors[...])


def front_kernel(plan, state, gates, angle, swaps, order, own, high, low):
    chunks = sent_rows(plan, scalars(swaps), scalars(order))
    chosen = one_hot(plan, [rows for rows, _ in chunks])
    core = lax.axis_index("mid") & 1
    mask = jnp.concatenate([(held == core).astype(jnp.float32) for _, held in chunks], 0)
    mask = jnp.concatenate([mask, mask], 1)
    outer = tuple(dot(chosen, part).astype(jnp.bfloat16) for part in split(gate(gates, 3)))
    inner = turn(gate(gates, 1), angle[...])
    merged = complex_product(outer, split(inner))
    own[...] = complex_product(split(merged * mask), split(state[...]))
    high[...], low[...] = split(merged * (1.0 - mask))


def send_kernel(plan, own, high, low, state, *sent):
    total = own[...] + complex_product((high[...], low[...]), split(state[...]))
    start = 0
    for ref in sent:
        ref[...] = total[start : start + ref.shape[0]]
        start += ref.shape[0]


def chain(factors):
    while len(factors) > 1:
        pairs = [factors[k : k + 2] for k in range(0, len(factors), 2)]
        factors = [
            complex_product(split(pair[0]), split(pair[1])) if len(pair) == 2 else pair[0]
            for pair in pairs
        ]
    return factors[0]


def right_kernel(plan, count, gates, phase_low, high, low):
    factors = [gate(gates, number) for number in range((count - 1) // 2 * 2, 2, -2)]
    value = chain(factors + [turn(gate(gates, 2), phase_low[...]), gate(gates, 0)])
    real, imag = value[:, : plan.rows], value[:, plan.rows :]
    high[...], low[...] = split(
        jnp.concatenate(
            [jnp.concatenate([real, -imag], 1), jnp.concatenate([imag, real], 1)], 0
        )
    )


def left_kernel(plan, count, gates, swaps, high, low):
    placed = one_hot(plan, received_rows(plan, scalars(swaps)))
    first = gate(gates, 5)
    first = [
        sum(dot(part, placed, True) for part in split(half))
        for half in (first[:, : plan.rows], first[:, plan.rows :])
    ]
    factors = [gate(gates, number) for number in range((count - 2) // 2 * 2 + 1, 5, -2)]
    high[...], low[...] = split(chain(factors + [jnp.concatenate(first, 1)]))


def back_kernel(plan, count, gates, phase_low, swaps, kept, *factors):
    del kept
    right_kernel(plan, count, gates, phase_low, *factors[:2])
    left_kernel(plan, count, gates, swaps, *factors[2:])


def right_only(plan, count, gates, phase_low, kept, *out):
    right_kernel(plan, count, gates, phase_low, *out)


def left_only(plan, count, gates, swaps, kept, *out):
    left_kernel(plan, count, gates, swaps, *out)


def sort_kernel(plan, *refs):
    give = refs[-1]
    for place, ref in enumerate(refs[: len(plan.shared)]):
        give[place * plan.chunk : (place + 1) * plan.chunk] = ref[plan.chunk :]


def kept_kernel(plan, count, gates, swaps, give, *refs):
    del give
    *parts, right_high, right_low, left_high, left_low, high, low = refs
    left_kernel(plan, count, gates, swaps, left_high, left_low)
    value = jnp.concatenate([ref[: plan.chunk] for ref in parts], 0)
    value = product(split(value), (right_high[...], right_low[...]), True)
    high[...], low[...] = split(value)


def last_kernel(plan, high, low, *refs):
    *parts, right_high, right_low, left_high, left_low, out = refs
    value = jnp.concatenate([ref[...] for ref in parts], 0)
    value = split(product(split(value), (right_high[...], right_low[...]), True))
    value = tuple(jnp.concatenate([a[...], b], 0) for a, b in zip((high, low), value))
    result = complex_product((left_high[...], left_low[...]), value)
    half = plan.rows
    out[0] = result[:, :half]
    out[1] = result[:, half:]


def call(kernel, shapes, args, specs, flops=0):
    args = [
        arg if spec is SSPEC else pltpu.with_memory_space_constraint(arg, spec.memory_space)
        for arg, spec in zip(args, specs)
    ]
    return pl.pallas_call(
        kernel,
        out_shape=[pltpu.VMEM(shape, dtype) for shape, dtype in shapes],
        in_specs=specs,
        out_specs=[VSPEC] * len(shapes),
        cost_estimate=pl.CostEstimate(flops=flops, bytes_accessed=1 << 17, transcendentals=0),
    )(*args)


def exchange(value, step=((0, 0, 0), (0, 0, 0)), flip=0):
    wides, mids, lows = (lax.axis_size(axis) for axis in AXES)
    pairs = []
    for wide in range(wides):
        for mid in range(mids):
            for low in range(lows):
                *offsets, low_part = step[mid & 1]
                to_wide = wide ^ offsets[2 * wide // wides]
                to = (to_wide * mids + (mid ^ flip)) * lows + (low ^ low_part)
                pairs.append(((wide * mids + mid) * lows + low, to))
    return lax.ppermute(value, AXES, pairs)


def merged_device(state, gates, phase_low, phase_mid, phase_top, swap_qubits, regroup_order):
    rows = gates.shape[-1]
    plan = Plan(rows, lax.axis_size("wide"))
    chunk = plan.chunk
    f32, bf16 = jnp.float32, jnp.bfloat16
    gates = gates.reshape(-1, rows, rows)
    swaps, order = swap_qubits.reshape(1, -1), regroup_order.reshape(1, -1)
    square = state.reshape(2, rows, rows)
    (factors,) = call(partial(phase_kernel, plan), [((8, rows), f32)], (phase_top,), (SSPEC,), BUSY)
    (turned,) = call(load_kernel, [((rows, 2 * rows), f32)], (square, factors), (VSPEC,) * 2)
    other = exchange(turned, flip=1)
    own, high, low = call(
        partial(front_kernel, plan),
        [((rows, 2 * rows), f32), ((rows, 2 * rows), bf16), ((rows, 2 * rows), bf16)],
        (turned, gates, phase_mid.reshape(1, rows), swaps, order),
        (VSPEC,) * 5,
    )
    shapes = [(chunk, 2 * rows)]
    shapes += [(2 * chunk if step in plan.shared else chunk, 2 * rows) for step in plan.steps]
    local, *sent = call(
        partial(send_kernel, plan),
        [(shape, f32) for shape in shapes],
        (own, high, low, other),
        (VSPEC,) * 4,
    )
    received = [exchange(value, step) for value, step in zip(sent, plan.steps)]
    right_high, right_low = call(
        partial(right_only, plan, gates.shape[0] // 2),
        [((2 * rows, 2 * rows), bf16)] * 2,
        (gates, phase_low.reshape(1, rows), local),
        (VSPEC,) * 3,
    )
    shared = [value for value, step in zip(received, plan.steps) if step in plan.shared]
    (give,) = call(
        partial(sort_kernel, plan),
        [((len(plan.shared) * chunk, 2 * rows), f32)],
        (*shared, right_low),
        (VSPEC,) * (len(shared) + 1),
    )
    given = exchange(give, flip=1)
    kept_rows = (1 + len(shared)) * chunk
    left_high, left_low, high, low = call(
        partial(kept_kernel, plan, gates.shape[0] // 2),
        [((rows, 2 * rows), bf16)] * 2 + [((kept_rows, 2 * rows), bf16)] * 2,
        (gates, swaps, give, local, *shared, right_high, right_low),
        (VSPEC,) * (len(shared) + 6),
        LONG,
    )
    direct = [value for value, step in zip(received, plan.steps) if step in plan.direct]
    args = (high, low, *direct, given, right_high, right_low, left_high, left_low)
    out = pl.pallas_call(
        partial(last_kernel, plan),
        out_shape=jax.ShapeDtypeStruct((2, rows, rows), f32),
        in_specs=[VSPEC] * len(args),
    )(*[pltpu.with_memory_space_constraint(arg, pltpu.VMEM) for arg in args])
    return out.reshape(state.shape)


def mate(value, axis, stride):
    mask = 2**stride
    pairs = [(source, source ^ mask) for source in range(lax.axis_size(axis))]
    return lax.ppermute(value, axis, pairs)


def gate_inner(vector, real_gate, imag_gate):

    def product(values, matrix):
        return jnp.einsum("...b,ab->...a", values, matrix, precision=HIGH)

    real_part, imag_part = (vector[0], vector[1])
    return jnp.stack(
        [
            product(real_part, real_gate) - product(imag_part, imag_gate),
            product(real_part, imag_gate) + product(imag_part, real_gate),
        ]
    )


def gate_outer(vector, real_gate, imag_gate):

    def product(values, matrix):
        return jnp.einsum("ab,rbc->rac", matrix, values, precision=HIGH)

    real_part, imag_part = (vector[0], vector[1])
    return jnp.stack(
        [
            product(real_part, real_gate) - product(imag_part, imag_gate),
            product(real_part, imag_gate) + product(imag_part, real_gate),
        ]
    )


def apply_gate(vector, gates, number, gate_len):
    if number % 2 == 0:
        result = gate_inner(vector.reshape(2, -1, gate_len), gates[number, 0], gates[number, 1])
    else:
        result = gate_outer(
            vector.reshape(2, -1, gate_len, gate_len), gates[number, 0], gates[number, 1]
        )
    return result.reshape(2, -1)


def half_rows(vector, offset, base, own_bit, local_len):
    counter = jnp.arange(4, dtype=jnp.int32)
    lower = counter & jnp.left_shift(1, offset) - 1
    higher = jnp.right_shift(counter, offset)
    row_index = jnp.left_shift(higher, offset + 1) | jnp.left_shift(1 - own_bit, offset) | lower
    blocks = vector.reshape(2, local_len >> base + 3, 8, 1 << base)
    return (blocks, row_index, jnp.take(blocks, row_index, axis=2))


def move_bits(vector, lower, upper, local_len):
    if lower == upper:
        return vector
    shaped = vector.reshape(2, local_len >> upper + 1, 2, 1 << upper - lower - 1, 2, 1 << lower)
    return jnp.swapaxes(shaped, 2, 4).reshape(2, local_len)


def general_device(state, gates, phase_low, phase_mid, phase_top, swap_qubits, regroup_order):
    local_len = state.shape[-1]
    gate_len = gates.shape[-1]
    gate_count = gates.shape[0]
    local_bits = local_len.bit_length() - 1
    upper_len = local_len // (gate_len * gate_len)
    wide_count = lax.axis_size("wide")
    wide_bits = wide_count.bit_length() - 1
    vector = apply_gate(state.reshape(2, -1), gates, 0, gate_len)
    vector = vector.reshape(2, upper_len, gate_len, gate_len)
    angle = (
        phase_top.reshape(upper_len)[:, None, None]
        + phase_mid[None, :, None]
        + phase_low[None, None, :]
    )
    cosine = jnp.cos(angle)
    sine_part = jnp.sin(angle)
    vector = jnp.stack(
        [vector[0] * cosine - vector[1] * sine_part, vector[0] * sine_part + vector[1] * cosine]
    ).reshape(2, -1)
    for number in range(1, 4):
        vector = apply_gate(vector, gates, number, gate_len)
    mid_bit = lax.axis_index("mid") & 1
    blocks, row_index, sent_half = half_rows(
        vector, swap_qubits[0], local_bits - 3, mid_bit, local_len
    )
    received = mate(sent_half, "mid", 0)
    vector = blocks.at[:, :, row_index].set(received).reshape(2, local_len)
    row_ids = jnp.arange(16, dtype=jnp.int32)[:, None]
    row_bits = jnp.right_shift(row_ids, jnp.arange(4, dtype=jnp.int32)[None, :]) & 1
    order_index = jnp.sum(jnp.left_shift(row_bits, regroup_order[None, :]), axis=1)
    vector = jnp.take(vector.reshape(2, 16, local_len // 16), order_index, axis=1).reshape(
        2, local_len
    )
    low_base = local_bits - wide_bits - 3
    target = low_base + 2
    branches = [
        partial(move_bits, lower=low_base + place, upper=target, local_len=local_len)
        for place in range(3)
    ]
    vector = lax.switch(swap_qubits[1], branches, vector)
    shaped = vector.reshape(2, wide_count, 2, local_len // (2 * wide_count))
    moved = lax.all_to_all(
        lax.all_to_all(shaped, "wide", split_axis=1, concat_axis=1, tiled=True),
        "low",
        split_axis=2,
        concat_axis=2,
        tiled=True,
    )
    vector = lax.switch(swap_qubits[1], branches, moved.reshape(2, local_len))
    for number in range(4, gate_count):
        vector = apply_gate(vector, gates, number, gate_len)
    return vector.reshape(state.shape)


def on_device(state, gates, *rest):
    rows = gates.shape[-1]
    sizes = [lax.axis_size(axis) for axis in AXES]
    base = rows.bit_length() - sizes[0].bit_length() - 3
    merged = state.shape[-1] == rows * rows and base >= 2 and min(sizes) >= 2
    return (merged_device if merged else general_device)(state, gates, *rest)


def solution(mesh):
    return jax.shard_map(
        on_device,
        mesh=mesh,
        in_specs=(
            P(None, "wide", "mid", "low", None),
            P(),
            P(),
            P(),
            P("wide", "mid", "low", None),
            P(),
            P(),
        ),
        out_specs=P(None, "wide", "mid", "low", None),
        check_vma=False,
    )
```
